512 devices in a mesh: chan: 64 (over z, x, core), seg: 8 (over y).
Axes of the slice: x: 4, y: 8, z: 8, core: 2. Of those that a mesh axis runs over, the one named last changes fastest.
Arguments:
- raw: bfloat16 [16, 8192, 1536], P('seg', 'chan'), may hold values from -300 to 300, as said below
- send_order: int32 [8192], P('chan'), may hold values from 0 to 127, as said below
- pair_first: int32 [16384], P('chan'), may hold values from 0 to 127, as said below
- pair_offset: int32 [16384], P('chan'), may hold values from 1 to 48
- pair_count: int32 [64], P('chan'), may hold values from 32 to 256, as said below
Outputs:
- stacks: float32 [16384, 256], P(('chan', 'seg'))
The draws below stay inside these ranges and needn't reach their ends.
Inputs may be any that keep to these rules, and one draw needn't show every extreme that they name: `send_order`: on each index p of chan the 128 entries are a permutation of 0 .. 127, the local stored channels; entries b * 2 .. b * 2 + 1 go to pair block b. `pair_first`: a position inside the owner's block; in the last block pair_first + pair_offset stays below 128, so a pair's second channel lies in its own block or the next. `pair_count`: some block is full in every draw. `raw`: channels differ in gain and spectral colour.
All inputs are finite; a program needn't handle non-finite values.
Results may differ from the reference program's by a relative error of at most 0.0077.
Values may be sent and summed in bfloat16 or wider, within the bound.
No kernel may reach another device: no remote copies, remote signals or barrier semaphores. Data moves between devices by JAX's collectives and lax.ppermute only.
A program may use at most 64 MiB of HBM per device.

```python
import math
import jax
import jax.numpy as jnp
from jax import lax

L = 1536
F = 512
BAND = 32
LAGS = 256
REACH = 48
CH_DEV = 128
OWN_CAP = 256
CHANNELS = 8192
SEGMENTS = 16
PAIRS = 16384
N_CHAN = 64


def draw_raw(key, part):
    keys = jax.random.split(key, 4)
    shape = (SEGMENTS, CHANNELS, L + 1)
    noise = jax.random.truncated_normal(keys[0], -5.0, 5.0, shape, jnp.float32)
    colour = jax.random.uniform(keys[1], (1, CHANNELS, 1), jnp.float32, -0.8, 0.8)
    chan_gain = jnp.exp(jax.random.uniform(keys[2], (1, CHANNELS, 1), jnp.float32, 0.0, math.log(10.0)))
    seg_gain = jnp.exp(jax.random.uniform(keys[3], (SEGMENTS, 1, 1), jnp.float32, 0.0, math.log(3.0)))
    return ((noise[..., 1:] + colour * noise[..., :-1]) * chan_gain * seg_gain).astype(jnp.bfloat16)


def draw_send_order(key, part):
    keys = jax.random.split(jax.random.fold_in(key, 7), N_CHAN)
    shuffled = jax.vmap(lambda single: jax.random.permutation(single, CH_DEV))(keys)
    return shuffled.reshape(N_CHAN * CH_DEV).astype(jnp.int32)


def draw_pair_first(key, part):
    picked = jax.random.randint(jax.random.fold_in(key, 11), (N_CHAN, OWN_CAP), 0, CH_DEV, jnp.int32)
    last_block = (jnp.arange(N_CHAN, dtype=jnp.int32) == N_CHAN - 1)[:, None]
    picked = jnp.where(last_block, picked % (CH_DEV - REACH), picked)
    return picked.reshape(N_CHAN * OWN_CAP)


def draw_pair_count(key, part):
    counts = jax.random.randint(jax.random.fold_in(key, 13), (N_CHAN,), OWN_CAP // 8, OWN_CAP + 1, jnp.int32)
    fullest = jax.random.randint(jax.random.fold_in(key, 17), (), 0, N_CHAN, jnp.int32)
    return jnp.where(jnp.arange(N_CHAN, dtype=jnp.int32) == fullest, OWN_CAP, counts).astype(jnp.int32)


def touch_ends(entries, own_key, low, largest):
    dims = entries.shape
    index_at = [jax.random.randint(jax.random.fold_in(own_key, axis), (), 0, dims[axis]) for axis in range(len(dims))]
    entries = entries.at[tuple(index_at)].set(low)
    longest = dims.index(max(dims))
    index_at[longest] = (index_at[longest] + 1) % dims[longest]
    return entries.at[tuple(index_at)].set(largest)


def setup_inputs(seed: int = 0) -> dict:
    key_list = jax.random.split(jax.random.key(seed), 6)
    raw = draw_raw(jax.random.fold_in(key_list[5], 71), 0)
    send_order = draw_send_order(jax.random.fold_in(key_list[5], 71), 0)
    pair_first = draw_pair_first(jax.random.fold_in(key_list[5], 71), 0)
    pair_offset = touch_ends(jax.random.randint(key_list[3], (PAIRS,), 1, REACH + 1), jax.random.fold_in(key_list[3], 1), 1, REACH).astype(jnp.int32)
    pair_count = draw_pair_count(jax.random.fold_in(key_list[5], 71), 0)
    return dict(raw=raw, send_order=send_order, pair_first=pair_first, pair_offset=pair_offset, pair_count=pair_count)


def forward_table():
    bins = 1 + jnp.arange(F, dtype=jnp.int32)
    samples = jnp.arange(L, dtype=jnp.int32)
    phase = (samples[:, None] * bins[None, :] % L).astype(jnp.float32) * (2.0 * math.pi / L)
    return (jnp.cos(phase).astype(jnp.bfloat16), (-jnp.sin(phase)).astype(jnp.bfloat16))

def band_matrix():
    bin_index = jnp.arange(F, dtype=jnp.int32)
    nearby = (jnp.abs(bin_index[:, None] - bin_index[None, :]) <= BAND).astype(jnp.float32)
    return nearby / lax.optimization_barrier(jnp.sum(nearby, axis=0, keepdims=True))

def inverse_table(factor):
    bins = 1 + jnp.arange(F, dtype=jnp.int32)
    lag_shift = jnp.arange(LAGS, dtype=jnp.int32) - LAGS // 2
    phase = (bins[:, None] * lag_shift[None, :] % L).astype(jnp.float32) * (2.0 * math.pi / L)
    return jnp.concatenate([jnp.cos(phase), -jnp.sin(phase)], axis=0) * factor

def whiten(real_part, imag_part, smoother):
    power = real_part * real_part + imag_part * imag_part
    smooth = jnp.dot(power, smoother, precision=lax.Precision.HIGHEST, preferred_element_type=jnp.float32)
    factor = lax.rsqrt(smooth + 1e-06)
    return jnp.concatenate([real_part * factor, imag_part * factor], axis=-1).astype(jnp.bfloat16)

def cross_spectra(left_rows, right_rows):
    left_re = left_rows[..., :F].astype(jnp.float32)
    left_im = left_rows[..., F:].astype(jnp.float32)
    right_re = right_rows[..., :F].astype(jnp.float32)
    right_im = right_rows[..., F:].astype(jnp.float32)
    return jnp.concatenate([left_re * right_re + left_im * right_im, left_im * right_re - left_re * right_im], axis=-1)

def reference(raw, send_order, pair_first, pair_offset, pair_count):
    group_size = CH_DEV // N_CHAN
    shifted = send_order.reshape(N_CHAN, N_CHAN, group_size) + (jnp.arange(N_CHAN, dtype=jnp.int32) * CH_DEV)[:, None, None]
    channel_order = jnp.transpose(shifted, (1, 0, 2)).reshape(CHANNELS)
    slot_ids = jnp.arange(PAIRS, dtype=jnp.int32)
    owners = slot_ids // OWN_CAP
    first_pos = owners * CH_DEV + pair_first
    second_pos = first_pos + pair_offset
    live_mask = (slot_ids % OWN_CAP < pair_count[owners]).astype(jnp.float32)
    first_src = channel_order[first_pos]
    second_src = channel_order[second_pos]
    smoother = band_matrix()
    cosines, sines = forward_table()

    def accumulate(running, segment):
        wave = segment.astype(jnp.float32)
        normed = (wave * lax.rsqrt(lax.optimization_barrier(jnp.mean(wave * wave, axis=-1, keepdims=True)) + 1e-05)).astype(jnp.bfloat16)
        real_part = jnp.dot(normed, cosines, preferred_element_type=jnp.float32)
        imag_part = jnp.dot(normed, sines, preferred_element_type=jnp.float32)
        white = whiten(real_part, imag_part, smoother)
        return (running + cross_spectra(white[first_src], white[second_src]), None)
    summed = lax.scan(accumulate, jnp.zeros((PAIRS, 2 * F), jnp.float32), raw)[0]
    stacked = summed * live_mask[:, None]
    lag_table = inverse_table(1.0 / math.sqrt(SEGMENTS * F))
    return jnp.dot(stacked, lag_table, precision=lax.Precision.HIGHEST, preferred_element_type=jnp.float32)
```

```python
import math

import jax
import jax.numpy as jnp
import numpy as np
from jax import lax
from jax.experimental import pallas as pl
from jax.experimental.pallas import tpu as pltpu
from jax.sharding import PartitionSpec as P

L = 1536
F = 512
BAND = 32
LAGS = 256
REACH = 48
COLS = 256
STEPS = 4
BF = jnp.bfloat16
F32 = jnp.float32


def forward_table():
    bins = 1 + np.arange(F)
    samples = np.arange(L)
    phase = (samples[:, None] * bins[None, :] % L).astype(np.float32) * np.float32(2.0 * math.pi / L)
    cosines = np.cos(phase).astype(BF).reshape(L, STEPS, F // STEPS)
    sines = (-np.sin(phase)).astype(BF).reshape(L, STEPS, F // STEPS)
    return np.ascontiguousarray(np.concatenate([cosines, sines], axis=-1).transpose(1, 0, 2))


def band_tables():
    bin_index = np.arange(F)
    nearby = np.abs(bin_index[:, None] - bin_index[None, :]) <= BAND
    return nearby.astype(BF), (1.0 / nearby.sum(axis=0, keepdims=True)).astype(np.float32)


def inverse_tables(factor):
    bins = 1 + np.arange(F)
    lag_shift = np.arange(LAGS) - LAGS // 2
    phase = (bins[:, None] * lag_shift[None, :] % L).astype(np.float64) * (2.0 * math.pi / L)
    table = (np.concatenate([np.cos(phase), -np.sin(phase)], axis=0) * factor).astype(np.float32)
    high = table.astype(BF)
    return high, (table - high.astype(np.float32)).astype(BF)


def dot(a, b):
    return jnp.dot(a, b, preferred_element_type=F32)


def spread_matrix(blocks, back):
    rows = blocks * 16
    r = lax.broadcasted_iota(jnp.int32, (rows, rows), 0)
    k = lax.broadcasted_iota(jnp.int32, (rows, rows), 1)
    mixed, apart = (k, r) if back else (r, k)
    p, cs, j = mixed // 16, (mixed % 16) // 2, mixed % 2
    return (apart == cs * (2 * blocks) + p * 2 + j).astype(F32).astype(BF)


def whiten_kernel(raw_ref, order_ref, table_ref, band_ref, inv_ref, out_ref, normed, real, imag, smooth):
    step = pl.program_id(0)
    width = F // STEPS

    @pl.when(step == 0)
    def _():
        wave = raw_ref[...].astype(F32)
        mean = jnp.sum(wave * wave, axis=-1, keepdims=True) * (1.0 / L)
        normed[...] = (wave * lax.rsqrt(mean + 1e-05)).astype(BF)
        smooth[...] = jnp.zeros_like(smooth)

    spec = dot(normed[...], table_ref[0])
    re, im = spec[:, :width], spec[:, width:]
    real[step] = re
    imag[step] = im
    power = re * re + im * im
    high = power.astype(BF)
    low = (power - high.astype(F32)).astype(BF)
    near = band_ref[...]
    smooth[...] += dot(high, near) + dot(low, near)

    @pl.when(step == STEPS - 1)
    def _():
        factor = lax.rsqrt(smooth[...] * inv_ref[...] + 1e-06)
        channels = lax.broadcasted_iota(jnp.int32, (128, 128), 0)
        pick = (channels == order_ref[...]).astype(F32).T.astype(BF)
        picked = []
        for s in range(2):
            rows = slice(s * 128, s * 128 + 128)
            parts = [real[i, rows] * factor[rows, i * width : (i + 1) * width] for i in range(STEPS)]
            parts += [imag[i, rows] * factor[rows, i * width : (i + 1) * width] for i in range(STEPS)]
            white = jnp.concatenate(parts, axis=1).astype(BF)
            picked.append(dot(pick, white).astype(BF))
        mix = spread_matrix(16, False)
        for b in range(4):
            stacked = jnp.concatenate(
                [
                    picked[s][b * 32 : b * 32 + 32, c * COLS : (c + 1) * COLS]
                    for c in range(4)
                    for s in range(2)
                ],
                axis=0,
            )
            out_ref[b * 16 : b * 16 + 16] = dot(mix, stacked).astype(BF).reshape(16, 16, COLS)


def whitened(raw, send_order):
    near, inv = band_tables()
    return pl.pallas_call(
        whiten_kernel,
        grid=(STEPS,),
        in_specs=[
            pl.BlockSpec((256, L), lambda i: (0, 0)),
            pl.BlockSpec((1, 128), lambda i: (0, 0)),
            pl.BlockSpec((1, L, COLS), lambda i: (i, 0, 0)),
            pl.BlockSpec((F // STEPS, F), lambda i: (i, 0)),
            pl.BlockSpec((1, F), lambda i: (0, 0)),
        ],
        out_specs=pl.BlockSpec((64, 16, COLS), lambda i: (0, 0, 0)),
        out_shape=jax.ShapeDtypeStruct((64, 16, COLS), BF),
        scratch_shapes=[
            pltpu.VMEM((256, L), BF),
            pltpu.VMEM((STEPS, 256, F // STEPS), F32),
            pltpu.VMEM((STEPS, 256, F // STEPS), F32),
            pltpu.VMEM((256, F), F32),
        ],
        compiler_params=pltpu.CompilerParams(vmem_limit_bytes=32 * 1024 * 1024),
        name="whiten",
    )(raw.reshape(256, L), send_order.reshape(1, 128), forward_table(), near, inv)


def pairs_kernel(own_ref, rim_ref, first_ref, offset_ref, count_ref, high_ref, low_ref, out_ref, rows_ref):
    apart = spread_matrix(16, True)
    for b in range(4):
        block = dot(apart, own_ref[b * 16 : b * 16 + 16].reshape(256, COLS)).astype(BF)
        for c in range(4):
            for s in range(2):
                at = (c * 2 + s) * 32
                rows_ref[s, c, b * 32 : b * 32 + 32] = block[at : at + 32]
    apart = spread_matrix(8, True)
    for b in range(3):
        block = dot(apart, rim_ref[b * 8 : b * 8 + 8].reshape(128, COLS)).astype(BF)
        for c in range(4):
            for s in range(2):
                at = (c * 2 + s) * 16
                rows_ref[s, c, 128 + b * 16 : 128 + b * 16 + 16] = block[at : at + 16]
    first = first_ref[...]
    second = first + offset_ref[...]
    slot = lax.broadcasted_iota(jnp.int32, (1, 256), 1)
    first = jnp.where(slot < count_ref[0], first, -1)
    left_at = lax.broadcasted_iota(jnp.int32, (128, 256), 0)
    left_pick = (left_at == first).astype(F32).T.astype(BF)
    right_at = lax.broadcasted_iota(jnp.int32, (176, 256), 0)
    right_pick = (right_at == second).astype(F32).T.astype(BF)
    total = jnp.zeros((256, LAGS), F32)
    for c in range(2):
        re = jnp.zeros((256, COLS), F32)
        im = jnp.zeros((256, COLS), F32)
        for s in range(2):
            a_re = dot(left_pick, rows_ref[s, c, :128])
            a_im = dot(left_pick, rows_ref[s, c + 2, :128])
            c_re = dot(right_pick, rows_ref[s, c])
            c_im = dot(right_pick, rows_ref[s, c + 2])
            re += a_re * c_re + a_im * c_im
            im += a_im * c_re - a_re * c_im
        for part, row in ((re, c * COLS), (im, (c + 2) * COLS)):
            high = part.astype(BF)
            low = (part - high.astype(F32)).astype(BF)
            table = high_ref[row : row + COLS]
            total += dot(high, table) + dot(low, table) + dot(high, low_ref[row : row + COLS])
    out_ref[...] = total.astype(BF)


def pair_lags(own, rim, pair_first, pair_offset, pair_count, factor):
    high, low = inverse_tables(factor)
    vmem = pl.BlockSpec(memory_space=pltpu.VMEM)
    return pl.pallas_call(
        pairs_kernel,
        in_specs=[vmem, vmem, vmem, vmem, pl.BlockSpec(memory_space=pltpu.SMEM), vmem, vmem],
        out_specs=vmem,
        out_shape=jax.ShapeDtypeStruct((256, LAGS), BF),
        scratch_shapes=[pltpu.VMEM((2, 4, 176, COLS), BF)],
        compiler_params=pltpu.CompilerParams(vmem_limit_bytes=32 * 1024 * 1024),
        name="pairs",
    )(own, rim, pair_first.reshape(1, 256), pair_offset.reshape(1, 256), pair_count, high, low)


def on_device(raw, send_order, pair_first, pair_offset, pair_count):
    seg_count = raw.shape[0]
    groups = lax.axis_size("seg")
    blocks = lax.axis_size("chan")
    sent = whitened(raw, send_order)
    own = lax.all_to_all(sent, "chan", split_axis=0, concat_axis=0, tiled=True)
    rim = lax.ppermute(own[: REACH // 2], "chan", [(i + 1, i) for i in range(blocks - 1)])
    lags = pair_lags(own, rim, pair_first, pair_offset, pair_count, 1.0 / math.sqrt(seg_count * groups * F))
    shares = lax.all_to_all(lags.reshape(groups, 256 // groups, LAGS), "seg", 0, 0, tiled=True)
    return jnp.sum(shares.astype(F32), axis=0)


def solution(mesh):
    return jax.shard_map(
        on_device,
        mesh=mesh,
        in_specs=(P("seg", "chan", None), P("chan"), P("chan"), P("chan"), P("chan")),
        out_specs=P(("chan", "seg"), None),
        check_vma=False,
    )
```

```python
import math

import jax
import jax.numpy as jnp
import numpy as np
from jax import lax
from jax.experimental import pallas as pl
from jax.experimental.pallas import tpu as pltpu
from jax.sharding import PartitionSpec as P

L = 1536
F = 512
BAND = 32
LAGS = 256
REACH = 48
COLS = 256
STEPS = 4
BF = jnp.bfloat16
F32 = jnp.float32


def forward_table():
    bins = 1 + np.arange(F)
    samples = np.arange(L)
    phase = (samples[:, None] * bins[None, :] % L).astype(np.float32) * np.float32(2.0 * math.pi / L)
    cosines = np.cos(phase).astype(BF).reshape(L, STEPS, F // STEPS)
    sines = (-np.sin(phase)).astype(BF).reshape(L, STEPS, F // STEPS)
    return np.ascontiguousarray(np.concatenate([cosines, sines], axis=-1).transpose(1, 0, 2))


def band_tables():
    bin_index = np.arange(F)
    nearby = np.abs(bin_index[:, None] - bin_index[None, :]) <= BAND
    return nearby.astype(BF), (1.0 / nearby.sum(axis=0, keepdims=True)).astype(np.float32)


def inverse_tables(factor):
    bins = 1 + np.arange(F)
    lag_shift = np.arange(LAGS) - LAGS // 2
    phase = (bins[:, None] * lag_shift[None, :] % L).astype(np.float64) * (2.0 * math.pi / L)
    table = (np.concatenate([np.cos(phase), -np.sin(phase)], axis=0) * factor).astype(np.float32)
    high = table.astype(BF)
    return high, (table - high.astype(np.float32)).astype(BF)


def dot(a, b):
    return jnp.dot(a, b, preferred_element_type=F32)


def spread_matrix(blocks, back):
    rows = blocks * 16
    r = lax.broadcasted_iota(jnp.int32, (rows, rows), 0)
    k = lax.broadcasted_iota(jnp.int32, (rows, rows), 1)
    mixed, apart = (k, r) if back else (r, k)
    p, cs, j = mixed // 16, (mixed % 16) // 2, mixed % 2
    return (apart == cs * (2 * blocks) + p * 2 + j).astype(F32).astype(BF)


def whiten_kernel(
    raw_hbm, order_hbm, table_hbm, band_hbm, inv_hbm, out_ref, raw_ref, order_ref, table_ref, band_ref, inv_ref, normed, sems
):
    width = F // STEPS
    half = F // 2
    copies = [pltpu.make_async_copy(raw_hbm.at[s], raw_ref.at[s], sems.at[s]) for s in range(2)]
    copies += [pltpu.make_async_copy(table_hbm.at[i], table_ref.at[i], sems.at[2 + i]) for i in range(STEPS)]
    copies += [
        pltpu.make_async_copy(band_hbm, band_ref, sems.at[2 + STEPS]),
        pltpu.make_async_copy(inv_hbm, inv_ref, sems.at[3 + STEPS]),
        pltpu.make_async_copy(order_hbm, order_ref, sems.at[4 + STEPS]),
    ]
    for copy in copies:
        copy.start()
    mix = spread_matrix(16, False)
    for s in range(2):
        copies[s].wait()
        wave = raw_ref[s].astype(F32)
        mean = jnp.sum(wave * wave, axis=-1, keepdims=True) * (1.0 / L)
        normed[s * 128 : s * 128 + 128] = (wave * lax.rsqrt(mean + 1e-05)).astype(BF)
    real, imag = [], []
    smooth = None
    for i in range(STEPS):
        copies[2 + i].wait()
        spec = dot(normed[...], table_ref[i])
        real.append(spec[:, :width])
        imag.append(spec[:, width:])
        if i == 1:
            copies[2 + STEPS].wait()
        if i % 2:
            power = jnp.concatenate([real[k] * real[k] + imag[k] * imag[k] for k in (i - 1, i)], axis=1)
            high = power.astype(BF)
            low = (power - high.astype(F32)).astype(BF)
            near = band_ref[(i // 2) * half : (i // 2 + 1) * half]
            part = dot(high, near) + dot(low, near)
            smooth = part if smooth is None else smooth + part
    for copy in copies[3 + STEPS :]:
        copy.wait()
    factor = lax.rsqrt(smooth * inv_ref[...] + 1e-06)
    channels = lax.broadcasted_iota(jnp.int32, (128, 128), 0)
    pick = (channels == order_ref[...]).astype(F32).T.astype(BF)
    picked = []
    for s in range(2):
        rows = slice(s * 128, s * 128 + 128)
        scaled = [x[i][rows] * factor[rows, i * width : (i + 1) * width] for x in (real, imag) for i in range(STEPS)]
        picked.append(dot(pick, jnp.concatenate(scaled, axis=1).astype(BF)).astype(BF))
    for b in range(4):
        stacked = jnp.concatenate(
            [picked[s][b * 32 : b * 32 + 32, c * COLS : (c + 1) * COLS] for c in range(4) for s in range(2)], axis=0
        )
        out_ref[b * 16 : b * 16 + 16] = dot(mix, stacked).astype(BF).reshape(16, 16, COLS)


def whitened(raw, send_order):
    near, inv = band_tables()
    hbm = pl.BlockSpec(memory_space=pltpu.HBM)
    return pl.pallas_call(
        whiten_kernel,
        in_specs=[hbm] * 5,
        out_specs=pl.BlockSpec(memory_space=pltpu.VMEM),
        out_shape=jax.ShapeDtypeStruct((64, 16, COLS), BF),
        scratch_shapes=[
            pltpu.VMEM((2, 128, L), BF),
            pltpu.VMEM((1, 128), jnp.int32),
            pltpu.VMEM((STEPS, L, COLS), BF),
            pltpu.VMEM((F, F), BF),
            pltpu.VMEM((1, F), F32),
            pltpu.VMEM((256, L), BF),
            pltpu.SemaphoreType.DMA((5 + STEPS,)),
        ],
        compiler_params=pltpu.CompilerParams(vmem_limit_bytes=32 * 1024 * 1024),
        name="whiten",
    )(raw, send_order.reshape(1, 128), forward_table(), near, inv)


def pairs_kernel(own_ref, rim_ref, first_ref, offset_ref, count_ref, high_ref, low_ref, out_ref, rows_ref):
    apart = spread_matrix(16, True)
    for b in range(4):
        block = dot(apart, own_ref[b * 16 : b * 16 + 16].reshape(256, COLS)).astype(BF)
        for c in range(4):
            for s in range(2):
                at = (c * 2 + s) * 32
                rows_ref[s, c, b * 32 : b * 32 + 32] = block[at : at + 32]
    apart = spread_matrix(8, True)
    for b in range(3):
        block = dot(apart, rim_ref[b * 8 : b * 8 + 8].reshape(128, COLS)).astype(BF)
        for c in range(4):
            for s in range(2):
                at = (c * 2 + s) * 16
                rows_ref[s, c, 128 + b * 16 : 128 + b * 16 + 16] = block[at : at + 16]
    first = first_ref[...]
    second = first + offset_ref[...]
    slot = lax.broadcasted_iota(jnp.int32, (1, 256), 1)
    first = jnp.where(slot < count_ref[0], first, -1)
    left_at = lax.broadcasted_iota(jnp.int32, (128, 256), 0)
    left_pick = (left_at == first).astype(F32).T.astype(BF)
    right_at = lax.broadcasted_iota(jnp.int32, (176, 256), 0)
    right_pick = (right_at == second).astype(F32).T.astype(BF)
    total = jnp.zeros((256, LAGS), F32)
    for c in range(2):
        re = jnp.zeros((256, COLS), F32)
        im = jnp.zeros((256, COLS), F32)
        for s in range(2):
            a_re = dot(left_pick, rows_ref[s, c, :128])
            a_im = dot(left_pick, rows_ref[s, c + 2, :128])
            c_re = dot(right_pick, rows_ref[s, c])
            c_im = dot(right_pick, rows_ref[s, c + 2])
            re += a_re * c_re + a_im * c_im
            im += a_im * c_re - a_re * c_im
        for part, row in ((re, c * COLS), (im, (c + 2) * COLS)):
            high = part.astype(BF)
            low = (part - high.astype(F32)).astype(BF)
            table = high_ref[row : row + COLS]
            total += dot(high, table) + dot(low, table) + dot(high, low_ref[row : row + COLS])
    out_ref[...] = total.astype(BF)


def pair_lags(own, rim, pair_first, pair_offset, pair_count, factor):
    high, low = inverse_tables(factor)
    vmem = pl.BlockSpec(memory_space=pltpu.VMEM)
    return pl.pallas_call(
        pairs_kernel,
        in_specs=[vmem, vmem, vmem, vmem, pl.BlockSpec(memory_space=pltpu.SMEM), vmem, vmem],
        out_specs=vmem,
        out_shape=jax.ShapeDtypeStruct((256, LAGS), BF),
        scratch_shapes=[pltpu.VMEM((2, 4, 176, COLS), BF)],
        compiler_params=pltpu.CompilerParams(vmem_limit_bytes=32 * 1024 * 1024),
        name="pairs",
    )(own, rim, pair_first.reshape(1, 256), pair_offset.reshape(1, 256), pair_count, high, low)


def on_device(raw, send_order, pair_first, pair_offset, pair_count):
    seg_count = raw.shape[0]
    groups = lax.axis_size("seg")
    blocks = lax.axis_size("chan")
    sent = whitened(raw, send_order)
    own = lax.all_to_all(sent, "chan", split_axis=0, concat_axis=0, tiled=True)
    rim = lax.ppermute(own[: REACH // 2], "chan", [(i + 1, i) for i in range(blocks - 1)])
    lags = pair_lags(own, rim, pair_first, pair_offset, pair_count, 1.0 / math.sqrt(seg_count * groups * F))
    shares = lax.all_to_all(lags.reshape(groups, 256 // groups, LAGS), "seg", 0, 0, tiled=True)
    return jnp.sum(shares.astype(F32), axis=0)


def solution(mesh):
    return jax.shard_map(
        on_device,
        mesh=mesh,
        in_specs=(P("seg", "chan", None), P("chan"), P("chan"), P("chan"), P("chan")),
        out_specs=P(("chan", "seg"), None),
        check_vma=False,
    )
```

```python
import math

import jax
import jax.numpy as jnp
import numpy as np
from jax import lax
from jax.experimental import pallas as pl
from jax.experimental.pallas import tpu as pltpu
from jax.sharding import PartitionSpec as P

L = 1536
F = 512
BAND = 32
LAGS = 256
REACH = 48
COLS = 256
STEPS = 4
BF = jnp.bfloat16
F32 = jnp.float32


def forward_table():
    bins = 1 + np.arange(F)
    samples = np.arange(L)
    phase = (samples[:, None] * bins[None, :] % L).astype(np.float32) * np.float32(2.0 * math.pi / L)
    cosines = np.cos(phase).astype(BF).reshape(L, STEPS, F // STEPS)
    sines = (-np.sin(phase)).astype(BF).reshape(L, STEPS, F // STEPS)
    return np.ascontiguousarray(np.concatenate([cosines, sines], axis=-1).transpose(1, 0, 2))


def band_tables():
    bin_index = np.arange(F)
    nearby = np.abs(bin_index[:, None] - bin_index[None, :]) <= BAND
    return nearby.astype(BF), (1.0 / nearby.sum(axis=0, keepdims=True)).astype(np.float32)


def inverse_tables(factor):
    bins = 1 + np.arange(F)
    lag_shift = np.arange(LAGS) - LAGS // 2
    phase = (bins[:, None] * lag_shift[None, :] % L).astype(np.float64) * (2.0 * math.pi / L)
    table = (np.concatenate([np.cos(phase), -np.sin(phase)], axis=0) * factor).astype(np.float32)
    high = table.astype(BF)
    return high, (table - high.astype(np.float32)).astype(BF)


def dot(a, b):
    return jnp.dot(a, b, preferred_element_type=F32)


def spread_matrix(blocks, back):
    rows = blocks * 16
    r = lax.broadcasted_iota(jnp.int32, (rows, rows), 0)
    k = lax.broadcasted_iota(jnp.int32, (rows, rows), 1)
    mixed, apart = (k, r) if back else (r, k)
    p, cs, j = mixed // 16, (mixed % 16) // 2, mixed % 2
    return (apart == cs * (2 * blocks) + p * 2 + j).astype(F32).astype(BF)


def whiten_kernel(
    raw_hbm, order_hbm, table_hbm, band_hbm, inv_hbm, out_ref, raw_ref, order_ref, table_ref, band_ref, inv_ref, normed, sems
):
    width = F // STEPS
    half = F // 2
    copies = [pltpu.make_async_copy(raw_hbm.at[s], raw_ref.at[s], sems.at[s]) for s in range(2)]
    copies += [pltpu.make_async_copy(table_hbm.at[i], table_ref.at[i], sems.at[2 + i]) for i in range(STEPS)]
    copies += [
        pltpu.make_async_copy(band_hbm, band_ref, sems.at[2 + STEPS]),
        pltpu.make_async_copy(inv_hbm, inv_ref, sems.at[3 + STEPS]),
        pltpu.make_async_copy(order_hbm, order_ref, sems.at[4 + STEPS]),
    ]
    for copy in copies:
        copy.start()
    mix = spread_matrix(16, False)
    for s in range(2):
        copies[s].wait()
        wave = raw_ref[s].astype(F32)
        mean = jnp.sum(wave * wave, axis=-1, keepdims=True) * (1.0 / L)
        normed[s * 128 : s * 128 + 128] = (wave * lax.rsqrt(mean + 1e-05)).astype(BF)
    real, imag = [], []
    smooth = None
    for i in range(STEPS):
        copies[2 + i].wait()
        spec = dot(normed[...], table_ref[i])
        real.append(spec[:, :width])
        imag.append(spec[:, width:])
        if i == 1:
            copies[2 + STEPS].wait()
        if i % 2:
            power = jnp.concatenate([real[k] * real[k] + imag[k] * imag[k] for k in (i - 1, i)], axis=1)
            high = power.astype(BF)
            low = (power - high.astype(F32)).astype(BF)
            near = band_ref[(i // 2) * half : (i // 2 + 1) * half]
            part = dot(high, near) + dot(low, near)
            smooth = part if smooth is None else smooth + part
    for copy in copies[3 + STEPS :]:
        copy.wait()
    factor = lax.rsqrt(smooth * inv_ref[...] + 1e-06)
    channels = lax.broadcasted_iota(jnp.int32, (128, 128), 0)
    pick = (channels == order_ref[...]).astype(F32).T.astype(BF)
    picked = []
    for s in range(2):
        rows = slice(s * 128, s * 128 + 128)
        scaled = [x[i][rows] * factor[rows, i * width : (i + 1) * width] for x in (real, imag) for i in range(STEPS)]
        picked.append(dot(pick, jnp.concatenate(scaled, axis=1).astype(BF)).astype(BF))
    for b in range(4):
        stacked = jnp.concatenate(
            [picked[s][b * 32 : b * 32 + 32, c * COLS : (c + 1) * COLS] for c in range(4) for s in range(2)], axis=0
        )
        out_ref[b * 16 : b * 16 + 16] = dot(mix, stacked).astype(BF).reshape(16, 16, COLS)


def in_hbm(x):
    return pltpu.with_memory_space_constraint(jnp.asarray(x), pltpu.HBM)


def whitened(raw, send_order):
    near, inv = band_tables()
    hbm = pl.BlockSpec(memory_space=pltpu.HBM)
    return pl.pallas_call(
        whiten_kernel,
        in_specs=[hbm] * 5,
        out_specs=pl.BlockSpec(memory_space=pltpu.VMEM),
        out_shape=jax.ShapeDtypeStruct((64, 16, COLS), BF),
        scratch_shapes=[
            pltpu.VMEM((2, 128, L), BF),
            pltpu.VMEM((1, 128), jnp.int32),
            pltpu.VMEM((STEPS, L, COLS), BF),
            pltpu.VMEM((F, F), BF),
            pltpu.VMEM((1, F), F32),
            pltpu.VMEM((256, L), BF),
            pltpu.SemaphoreType.DMA((5 + STEPS,)),
        ],
        compiler_params=pltpu.CompilerParams(vmem_limit_bytes=32 * 1024 * 1024),
        name="whiten",
    )(*(in_hbm(x) for x in (raw, send_order.reshape(1, 128), forward_table(), near, inv)))


def pairs_kernel(own_ref, rim_ref, first_ref, offset_ref, count_ref, high_ref, low_ref, out_ref, rows_ref):
    apart = spread_matrix(16, True)
    for b in range(4):
        block = dot(apart, own_ref[b * 16 : b * 16 + 16].reshape(256, COLS)).astype(BF)
        for c in range(4):
            for s in range(2):
                at = (c * 2 + s) * 32
                rows_ref[s, c, b * 32 : b * 32 + 32] = block[at : at + 32]
    apart = spread_matrix(8, True)
    for b in range(3):
        block = dot(apart, rim_ref[b * 8 : b * 8 + 8].reshape(128, COLS)).astype(BF)
        for c in range(4):
            for s in range(2):
                at = (c * 2 + s) * 16
                rows_ref[s, c, 128 + b * 16 : 128 + b * 16 + 16] = block[at : at + 16]
    first = first_ref[...]
    second = first + offset_ref[...]
    slot = lax.broadcasted_iota(jnp.int32, (1, 256), 1)
    first = jnp.where(slot < count_ref[0], first, -1)
    left_at = lax.broadcasted_iota(jnp.int32, (128, 256), 0)
    left_pick = (left_at == first).astype(F32).T.astype(BF)
    right_at = lax.broadcasted_iota(jnp.int32, (176, 256), 0)
    right_pick = (right_at == second).astype(F32).T.astype(BF)
    total = jnp.zeros((256, LAGS), F32)
    for c in range(2):
        re = jnp.zeros((256, COLS), F32)
        im = jnp.zeros((256, COLS), F32)
        for s in range(2):
            a_re = dot(left_pick, rows_ref[s, c, :128])
            a_im = dot(left_pick, rows_ref[s, c + 2, :128])
            c_re = dot(right_pick, rows_ref[s, c])
            c_im = dot(right_pick, rows_ref[s, c + 2])
            re += a_re * c_re + a_im * c_im
            im += a_im * c_re - a_re * c_im
        for part, row in ((re, c * COLS), (im, (c + 2) * COLS)):
            high = part.astype(BF)
            low = (part - high.astype(F32)).astype(BF)
            table = high_ref[row : row + COLS]
            total += dot(high, table) + dot(low, table) + dot(high, low_ref[row : row + COLS])
    out_ref[...] = total.astype(BF)


def pair_lags(own, rim, pair_first, pair_offset, pair_count, factor):
    high, low = inverse_tables(factor)
    vmem = pl.BlockSpec(memory_space=pltpu.VMEM)
    return pl.pallas_call(
        pairs_kernel,
        in_specs=[vmem, vmem, vmem, vmem, pl.BlockSpec(memory_space=pltpu.SMEM), vmem, vmem],
        out_specs=vmem,
        out_shape=jax.ShapeDtypeStruct((256, LAGS), BF),
        scratch_shapes=[pltpu.VMEM((2, 4, 176, COLS), BF)],
        compiler_params=pltpu.CompilerParams(vmem_limit_bytes=32 * 1024 * 1024),
        name="pairs",
    )(own, rim, pair_first.reshape(1, 256), pair_offset.reshape(1, 256), pair_count, high, low)


def on_device(raw, send_order, pair_first, pair_offset, pair_count):
    seg_count = raw.shape[0]
    groups = lax.axis_size("seg")
    blocks = lax.axis_size("chan")
    sent = whitened(raw, send_order)
    own = lax.all_to_all(sent, "chan", split_axis=0, concat_axis=0, tiled=True)
    rim = lax.ppermute(own[: REACH // 2], "chan", [(i + 1, i) for i in range(blocks - 1)])
    lags = pair_lags(own, rim, pair_first, pair_offset, pair_count, 1.0 / math.sqrt(seg_count * groups * F))
    shares = lax.all_to_all(lags.reshape(groups, 256 // groups, LAGS), "seg", 0, 0, tiled=True)
    return jnp.sum(shares.astype(F32), axis=0)


def solution(mesh):
    return jax.shard_map(
        on_device,
        mesh=mesh,
        in_specs=(P("seg", "chan", None), P("chan"), P("chan"), P("chan"), P("chan")),
        out_specs=P(("chan", "seg"), None),
        check_vma=False,
    )
```

```python
import math

import jax
import jax.numpy as jnp
import numpy as np
from jax import lax
from jax.experimental import pallas as pl
from jax.experimental.pallas import tpu as pltpu
from jax.sharding import PartitionSpec as P

L = 1536
F = 512
BAND = 32
LAGS = 256
REACH = 48
COLS = 256
STEPS = 4
BF = jnp.bfloat16
F32 = jnp.float32


BINS = (1 + np.arange(STEPS)[:, None] + STEPS * np.arange(F // STEPS)[None, :]).reshape(F)


def forward_table():
    quarter = L // 4
    phase = (np.arange(quarter)[:, None] * BINS[None, :] % L).astype(np.float32) * np.float32(2.0 * math.pi / L)
    cosines = np.cos(phase).astype(BF).reshape(quarter, STEPS, F // STEPS)
    sines = (-np.sin(phase)).astype(BF).reshape(quarter, STEPS, F // STEPS)
    return np.ascontiguousarray(np.concatenate([cosines, sines], axis=-1).transpose(1, 0, 2))


def inverse_tables(factor):
    bins = BINS
    lag_shift = np.arange(LAGS) - LAGS // 2
    phase = (bins[:, None] * lag_shift[None, :] % L).astype(np.float64) * (2.0 * math.pi / L)
    table = (np.concatenate([np.cos(phase), -np.sin(phase)], axis=0) * factor).astype(np.float32)
    high = table.astype(BF)
    return high, (table - high.astype(np.float32)).astype(BF)


def dot(a, b):
    return jnp.dot(a, b, preferred_element_type=F32)


def spread_matrix(blocks, back):
    rows = blocks * 16
    shape = (1, rows) if back else (rows, 1)
    mixed = lax.broadcasted_iota(jnp.int32, shape, 1 if back else 0)
    target = (mixed % 16) // 2 * (2 * blocks) + mixed // 16 * 2 + mixed % 2
    apart = lax.broadcasted_iota(jnp.int32, (rows, rows), 0 if back else 1)
    return (apart == target).astype(F32).astype(BF)


def split(x):
    high = x.astype(BF)
    return high, (x - high.astype(F32)).astype(BF)


def fold(normed, even, odd, first_row):
    quarter = L // 4
    x0, x1, x2, x3 = (normed[:, i * quarter : (i + 1) * quarter] for i in range(4))
    even0, even1 = x0 + x2, x1 + x3
    count = normed.shape[0]
    upper, lower = slice(first_row, first_row + count), slice(first_row + 256, first_row + 256 + count)
    for at, value in enumerate((even0 - even1, even0 + even1)):
        even[at, upper], even[at, lower] = split(value)
    for side, value in enumerate((x0 - x2, x1 - x3)):
        columns = slice(side * quarter, (side + 1) * quarter)
        odd[upper, columns], odd[lower, columns] = split(value)


def whiten_kernel(raw_hbm, order_hbm, table_hbm, out_ref, raw_ref, order_ref, table_ref, even, odd, sems):
    width = F // STEPS
    half = F // 2
    quarter = L // 4
    visit = (0, 2, 1, 3)
    raw_copies = [pltpu.make_async_copy(raw_hbm.at[s], raw_ref.at[s], sems.at[s]) for s in range(2)]
    table_copies = {
        i: pltpu.make_async_copy(table_hbm.at[i], table_ref.at[i, :quarter], sems.at[2 + i]) for i in visit
    }
    order_copy = pltpu.make_async_copy(order_hbm, order_ref, sems.at[2 + STEPS])
    for copy in (*raw_copies, *table_copies.values(), order_copy):
        copy.start()
    mix = spread_matrix(16, False)

    def bin_at(position):
        return (position % width) * STEPS + position // width + 1

    bin_row = bin_at(lax.broadcasted_iota(jnp.int32, (F, 1), 0))
    bin_line = bin_at(lax.broadcasted_iota(jnp.int32, (1, F), 1))
    near = (jnp.abs(bin_row - bin_line) <= BAND).astype(F32).astype(BF)
    count = jnp.minimum(bin_line + BAND, F) - jnp.maximum(bin_line - BAND, 1) + 1
    share = 1.0 / count.astype(F32)

    for s in range(2):
        raw_copies[s].wait()
        for r in range(0, 128, 32):
            wave = raw_ref[s, r : r + 32].astype(F32)
            mean = jnp.sum(wave * wave, axis=-1, keepdims=True) * (1.0 / L)
            normed = (wave * lax.rsqrt(mean + 1e-05)).astype(BF).astype(F32)
            fold(normed, even, odd, s * 128 + r)
    for i in (0, 2):
        table_copies[i].wait()
        cosines = table_ref[i, :quarter, :width]
        sines = table_ref[i, :quarter, width:]
        table_ref[i, quarter:, :width] = sines if i == 0 else -sines
        table_ref[i, quarter:, width:] = -cosines if i == 0 else cosines
    real, imag = {}, {}
    smooth = None
    for i in visit:
        if i % 2:
            table_copies[i].wait()
            both = dot(even[i // 2], table_ref[i, :quarter])
        else:
            both = dot(odd[...], table_ref[i])
        spec = both[:256] + both[256:]
        real[i] = spec[:, :width]
        imag[i] = spec[:, width:]
    for pair in ((0, 1), (2, 3)):
        power = jnp.concatenate([real[k] * real[k] + imag[k] * imag[k] for k in pair], axis=1)
        high, low = split(power)
        rows = near[pair[0] * width : pair[0] * width + half]
        part = dot(high, rows) + dot(low, rows)
        smooth = part if smooth is None else smooth + part
    order_copy.wait()
    factor = lax.rsqrt(smooth * share + 1e-06)
    channels = lax.broadcasted_iota(jnp.int32, (128, 128), 0)
    pick = (channels == order_ref[...]).astype(F32).T.astype(BF)
    picked = []
    for s in range(2):
        rows = slice(s * 128, s * 128 + 128)
        scaled = [x[i][rows] * factor[rows, i * width : (i + 1) * width] for x in (real, imag) for i in range(STEPS)]
        picked.append(dot(pick, jnp.concatenate(scaled, axis=1).astype(BF)).astype(BF))
    for b in range(4):
        stacked = jnp.concatenate(
            [picked[s][b * 32 : b * 32 + 32, c * COLS : (c + 1) * COLS] for c in range(4) for s in range(2)], axis=0
        )
        out_ref[b * 16 : b * 16 + 16] = dot(mix, stacked).astype(BF).reshape(16, 16, COLS)


def in_hbm(x):
    return pltpu.with_memory_space_constraint(jnp.asarray(x), pltpu.HBM)


def whitened(raw, send_order):
    hbm = pl.BlockSpec(memory_space=pltpu.HBM)
    return pl.pallas_call(
        whiten_kernel,
        in_specs=[hbm] * 3,
        out_specs=pl.BlockSpec(memory_space=pltpu.VMEM),
        out_shape=jax.ShapeDtypeStruct((64, 16, COLS), BF),
        scratch_shapes=[
            pltpu.VMEM((2, 128, L), BF),
            pltpu.VMEM((1, 128), jnp.int32),
            pltpu.VMEM((STEPS, L // 2, COLS), BF),
            pltpu.VMEM((2, 512, L // 4), BF),
            pltpu.VMEM((512, L // 2), BF),
            pltpu.SemaphoreType.DMA((3 + STEPS,)),
        ],
        compiler_params=pltpu.CompilerParams(vmem_limit_bytes=32 * 1024 * 1024),
        name="whiten",
    )(*(in_hbm(x) for x in (raw, send_order.reshape(1, 128), forward_table())))


def pairs_kernel(own_ref, rim_ref, first_ref, offset_ref, count_ref, high_ref, low_ref, out_ref, rows_ref):
    apart = spread_matrix(16, True)
    for b in range(4):
        block = dot(apart, own_ref[b * 16 : b * 16 + 16].reshape(256, COLS)).astype(BF)
        for c in range(4):
            for s in range(2):
                at = (c * 2 + s) * 32
                rows_ref[s, c, b * 32 : b * 32 + 32] = block[at : at + 32]
    apart = spread_matrix(8, True)
    for b in range(3):
        block = dot(apart, rim_ref[b * 8 : b * 8 + 8].reshape(128, COLS)).astype(BF)
        for c in range(4):
            for s in range(2):
                at = (c * 2 + s) * 16
                rows_ref[s, c, 128 + b * 16 : 128 + b * 16 + 16] = block[at : at + 16]
    first = first_ref[...]
    second = first + offset_ref[...]
    slot = lax.broadcasted_iota(jnp.int32, (1, 256), 1)
    first = jnp.where(slot < count_ref[0], first, -1)
    left_at = lax.broadcasted_iota(jnp.int32, (128, 256), 0)
    left_pick = (left_at == first).astype(F32).T.astype(BF)
    right_at = lax.broadcasted_iota(jnp.int32, (176, 256), 0)
    right_pick = (right_at == second).astype(F32).T.astype(BF)
    total = jnp.zeros((256, LAGS), F32)
    for c in range(2):
        re = jnp.zeros((256, COLS), F32)
        im = jnp.zeros((256, COLS), F32)
        for s in range(2):
            a_re = dot(left_pick, rows_ref[s, c, :128])
            a_im = dot(left_pick, rows_ref[s, c + 2, :128])
            c_re = dot(right_pick, rows_ref[s, c])
            c_im = dot(right_pick, rows_ref[s, c + 2])
            re += a_re * c_re + a_im * c_im
            im += a_im * c_re - a_re * c_im
        for part, row in ((re, c * COLS), (im, (c + 2) * COLS)):
            high = part.astype(BF)
            low = (part - high.astype(F32)).astype(BF)
            table = high_ref[row : row + COLS]
            total += dot(high, table) + dot(low, table) + dot(high, low_ref[row : row + COLS])
    out_ref[...] = total.astype(BF)


def pair_lags(own, rim, pair_first, pair_offset, pair_count, factor):
    high, low = inverse_tables(factor)
    vmem = pl.BlockSpec(memory_space=pltpu.VMEM)
    return pl.pallas_call(
        pairs_kernel,
        in_specs=[vmem, vmem, vmem, vmem, pl.BlockSpec(memory_space=pltpu.SMEM), vmem, vmem],
        out_specs=vmem,
        out_shape=jax.ShapeDtypeStruct((256, LAGS), BF),
        scratch_shapes=[pltpu.VMEM((2, 4, 176, COLS), BF)],
        compiler_params=pltpu.CompilerParams(vmem_limit_bytes=32 * 1024 * 1024),
        name="pairs",
    )(own, rim, pair_first.reshape(1, 256), pair_offset.reshape(1, 256), pair_count, high, low)


def on_device(raw, send_order, pair_first, pair_offset, pair_count):
    seg_count = raw.shape[0]
    groups = lax.axis_size("seg")
    blocks = lax.axis_size("chan")
    sent = whitened(raw, send_order)
    own = lax.all_to_all(sent, "chan", split_axis=0, concat_axis=0, tiled=True)
    rim = lax.ppermute(own[: REACH // 2], "chan", [(i + 1, i) for i in range(blocks - 1)])
    lags = pair_lags(own, rim, pair_first, pair_offset, pair_count, 1.0 / math.sqrt(seg_count * groups * F))
    shares = lax.all_to_all(lags.reshape(groups, 256 // groups, LAGS), "seg", 0, 0, tiled=True)
    return jnp.sum(shares.astype(F32), axis=0)


def solution(mesh):
    return jax.shard_map(
        on_device,
        mesh=mesh,
        in_specs=(P("seg", "chan", None), P("chan"), P("chan"), P("chan"), P("chan")),
        out_specs=P(("chan", "seg"), None),
        check_vma=False,
    )
```

```python
import math

import jax
import jax.numpy as jnp
import numpy as np
from jax import lax
from jax.experimental import pallas as pl
from jax.experimental.pallas import tpu as pltpu
from jax.sharding import PartitionSpec as P

L = 1536
F = 512
BAND = 32
LAGS = 256
REACH = 48
COLS = 256
STEPS = 4
BF = jnp.bfloat16
F32 = jnp.float32


BINS = (1 + np.arange(STEPS)[:, None] + STEPS * np.arange(F // STEPS)[None, :]).reshape(F)


def forward_table():
    quarter = L // 4
    phase = (np.arange(quarter)[:, None] * BINS[None, :] % L).astype(np.float32) * np.float32(2.0 * math.pi / L)
    cosines = np.cos(phase).astype(BF).reshape(quarter, STEPS, F // STEPS)
    sines = (-np.sin(phase)).astype(BF).reshape(quarter, STEPS, F // STEPS)
    return np.ascontiguousarray(np.concatenate([cosines, sines], axis=-1).transpose(1, 0, 2))


def inverse_tables(factor):
    bins = BINS
    lag_shift = np.arange(LAGS) - LAGS // 2
    phase = (bins[:, None] * lag_shift[None, :] % L).astype(np.float64) * (2.0 * math.pi / L)
    table = (np.concatenate([np.cos(phase), -np.sin(phase)], axis=0) * factor).astype(np.float32)
    high = table.astype(BF)
    return high, (table - high.astype(np.float32)).astype(BF)


def dot(a, b):
    return jnp.dot(a, b, preferred_element_type=F32)


def spread_matrix(blocks, back):
    rows = blocks * 16
    shape = (1, rows) if back else (rows, 1)
    mixed = lax.broadcasted_iota(jnp.int32, shape, 1 if back else 0)
    target = (mixed % 16) // 2 * (2 * blocks) + mixed // 16 * 2 + mixed % 2
    apart = lax.broadcasted_iota(jnp.int32, (rows, rows), 0 if back else 1)
    return (apart == target).astype(F32).astype(BF)


def split(x):
    high = x.astype(BF)
    return high, (x - high.astype(F32)).astype(BF)


def fold(normed, even, odd, first_row):
    quarter = L // 4
    x0, x1, x2, x3 = (normed[:, i * quarter : (i + 1) * quarter] for i in range(4))
    even0, even1 = x0 + x2, x1 + x3
    count = normed.shape[0]
    upper, lower = slice(first_row, first_row + count), slice(first_row + 256, first_row + 256 + count)
    for at, value in enumerate((even0 - even1, even0 + even1)):
        even[at, upper], even[at, lower] = split(value)
    for side, value in enumerate((x0 - x2, x1 - x3)):
        columns = slice(side * quarter, (side + 1) * quarter)
        odd[upper, columns], odd[lower, columns] = split(value)


def whiten_kernel(raw_hbm, order_hbm, table_hbm, out_ref, raw_ref, order_ref, table_ref, even, odd, sems):
    width = F // STEPS
    half = F // 2
    quarter = L // 4
    visit = (0, 2, 1, 3)
    raw_copies = [pltpu.make_async_copy(raw_hbm.at[s], raw_ref.at[s], sems.at[s]) for s in range(2)]
    table_copies = {
        i: pltpu.make_async_copy(table_hbm.at[i], table_ref.at[i, :quarter], sems.at[2 + i]) for i in visit
    }
    order_copy = pltpu.make_async_copy(order_hbm, order_ref, sems.at[2 + STEPS])
    for copy in (*raw_copies, *table_copies.values(), order_copy):
        copy.start()
    mix = spread_matrix(16, False)

    def bin_at(position):
        return (position % width) * STEPS + position // width + 1

    bin_row = bin_at(lax.broadcasted_iota(jnp.int32, (F, 1), 0))
    bin_line = bin_at(lax.broadcasted_iota(jnp.int32, (1, F), 1))
    near = (jnp.abs(bin_row - bin_line) <= BAND).astype(F32).astype(BF)
    count = jnp.minimum(bin_line + BAND, F) - jnp.maximum(bin_line - BAND, 1) + 1
    share = 1.0 / count.astype(F32)

    for s in range(2):
        raw_copies[s].wait()
        for r in range(0, 128, 32):
            wave = raw_ref[s, r : r + 32].astype(F32)
            mean = jnp.sum(wave * wave, axis=-1, keepdims=True) * (1.0 / L)
            normed = (wave * lax.rsqrt(mean + 1e-05)).astype(BF).astype(F32)
            fold(normed, even, odd, s * 128 + r)
    for i in (0, 2):
        table_copies[i].wait()
        cosines = table_ref[i, :quarter, :width]
        sines = table_ref[i, :quarter, width:]
        table_ref[i, quarter:, :width] = sines if i == 0 else -sines
        table_ref[i, quarter:, width:] = -cosines if i == 0 else cosines
    real, imag = {}, {}
    smooth = None
    for i in visit:
        if i % 2:
            table_copies[i].wait()
            both = dot(even[i // 2], table_ref[i, :quarter])
        else:
            both = dot(odd[...], table_ref[i])
        spec = both[:256] + both[256:]
        real[i] = spec[:, :width]
        imag[i] = spec[:, width:]
    for pair in ((0, 1), (2, 3)):
        power = jnp.concatenate([real[k] * real[k] + imag[k] * imag[k] for k in pair], axis=1)
        high, low = split(power)
        rows = near[pair[0] * width : pair[0] * width + half]
        part = dot(high, rows) + dot(low, rows)
        smooth = part if smooth is None else smooth + part
    order_copy.wait()
    factor = lax.rsqrt(smooth * share + 1e-06)
    channels = lax.broadcasted_iota(jnp.int32, (128, 128), 0)
    pick = (channels == order_ref[...]).astype(F32).T.astype(BF)
    picked = []
    for s in range(2):
        rows = slice(s * 128, s * 128 + 128)
        scaled = [x[i][rows] * factor[rows, i * width : (i + 1) * width] for x in (real, imag) for i in range(STEPS)]
        picked.append(dot(pick, jnp.concatenate(scaled, axis=1).astype(BF)).astype(BF))
    for b in range(4):
        stacked = jnp.concatenate(
            [picked[s][b * 32 : b * 32 + 32, c * COLS : (c + 1) * COLS] for c in range(4) for s in range(2)], axis=0
        )
        out_ref[b * 16 : b * 16 + 16] = dot(mix, stacked).astype(BF).reshape(16, 16, COLS)


def in_hbm(x):
    return pltpu.with_memory_space_constraint(jnp.asarray(x), pltpu.HBM)


def whitened(raw, send_order):
    hbm = pl.BlockSpec(memory_space=pltpu.HBM)
    return pl.pallas_call(
        whiten_kernel,
        in_specs=[hbm] * 3,
        out_specs=pl.BlockSpec(memory_space=pltpu.VMEM),
        out_shape=jax.ShapeDtypeStruct((64, 16, COLS), BF),
        scratch_shapes=[
            pltpu.VMEM((2, 128, L), BF),
            pltpu.VMEM((1, 128), jnp.int32),
            pltpu.VMEM((STEPS, L // 2, COLS), BF),
            pltpu.VMEM((2, 512, L // 4), BF),
            pltpu.VMEM((512, L // 2), BF),
            pltpu.SemaphoreType.DMA((3 + STEPS,)),
        ],
        compiler_params=pltpu.CompilerParams(vmem_limit_bytes=32 * 1024 * 1024),
        name="whiten",
    )(*(in_hbm(x) for x in (raw, send_order.reshape(1, 128), forward_table())))


def gather_kernel(
    own_ref, count_ref, first_hbm, offset_hbm, high_hbm, low_hbm,
    left_ref, right_ref, pick_ref, high_ref, low_ref,
    rows_ref, first_ref, offset_ref, sems,
):
    moves = ((first_hbm, first_ref), (offset_hbm, offset_ref), (high_hbm, high_ref), (low_hbm, low_ref))
    copies = [pltpu.make_async_copy(src, dst, sems.at[i]) for i, (src, dst) in enumerate(moves)]
    for copy in copies:
        copy.start()
    apart = spread_matrix(16, True)
    for b in range(4):
        block = dot(apart, own_ref[b * 16 : b * 16 + 16].reshape(256, COLS)).astype(BF)
        for c in range(4):
            for s in range(2):
                at = (c * 2 + s) * 32
                rows_ref[s, c, b * 32 : b * 32 + 32] = block[at : at + 32]
    for copy in copies[:2]:
        copy.wait()
    first = first_ref[...]
    second = first + offset_ref[...]
    slot = lax.broadcasted_iota(jnp.int32, (1, 256), 1)
    live_first = jnp.where(slot < count_ref[0], first, -1)
    at = lax.broadcasted_iota(jnp.int32, (128, 256), 0)
    left_pick = (at == live_first).astype(F32).T.astype(BF)
    right_pick = (at == second).astype(F32).T.astype(BF)
    pick_ref[...] = (at + 128 == second).astype(F32).T.astype(BF)
    for s in range(2):
        for c in range(4):
            rows = rows_ref[s, c]
            left_ref[s, c] = dot(left_pick, rows).astype(BF)
            right_ref[s, c] = dot(right_pick, rows).astype(BF)
    for copy in copies[2:]:
        copy.wait()


def gathered(own, pair_first, pair_offset, pair_count, factor):
    high, low = inverse_tables(factor)
    vmem = pl.BlockSpec(memory_space=pltpu.VMEM)
    hbm = pl.BlockSpec(memory_space=pltpu.HBM)
    rows = jax.ShapeDtypeStruct((2, 4, 256, COLS), BF)
    table = jax.ShapeDtypeStruct((2 * F, LAGS), BF)
    return pl.pallas_call(
        gather_kernel,
        in_specs=[vmem, pl.BlockSpec(memory_space=pltpu.SMEM)] + [hbm] * 4,
        out_specs=[vmem] * 5,
        out_shape=[rows, rows, jax.ShapeDtypeStruct((256, 128), BF), table, table],
        scratch_shapes=[
            pltpu.VMEM((2, 4, 128, COLS), BF),
            pltpu.VMEM((1, 256), jnp.int32),
            pltpu.VMEM((1, 256), jnp.int32),
            pltpu.SemaphoreType.DMA((4,)),
        ],
        compiler_params=pltpu.CompilerParams(vmem_limit_bytes=32 * 1024 * 1024),
        name="gather",
    )(own, pair_count, *(in_hbm(x) for x in (pair_first.reshape(1, 256), pair_offset.reshape(1, 256), high, low)))


def pairs_kernel(rim_ref, left_ref, right_ref, pick_ref, high_ref, low_ref, out_ref):
    apart = spread_matrix(8, True)
    blocks = [dot(apart, rim_ref[b * 8 : b * 8 + 8].reshape(128, COLS)).astype(BF) for b in range(3)]
    pick = pick_ref[:, :REACH]

    def right(s, c):
        at = (c * 2 + s) * 16
        rim_rows = jnp.concatenate([block[at : at + 16] for block in blocks], axis=0)
        return right_ref[s, c].astype(F32) + dot(pick, rim_rows)

    highs, lows = {}, {}
    for c in range(2):
        re = im = None
        for s in range(2):
            a_re, a_im = left_ref[s, c].astype(F32), left_ref[s, c + 2].astype(F32)
            c_re, c_im = right(s, c), right(s, c + 2)
            one, two = a_re * c_re + a_im * c_im, a_im * c_re - a_re * c_im
            re = one if re is None else re + one
            im = two if im is None else im + two
        highs[c], lows[c] = split(re)
        highs[c + 2], lows[c + 2] = split(im)
    high = jnp.concatenate([highs[c] for c in range(4)], axis=1)
    low = jnp.concatenate([lows[c] for c in range(4)], axis=1)
    total = dot(high, high_ref[...]) + dot(low, high_ref[...]) + dot(high, low_ref[...])
    out_ref[...] = total.astype(BF)


def pair_lags(rim, parts):
    vmem = pl.BlockSpec(memory_space=pltpu.VMEM)
    return pl.pallas_call(
        pairs_kernel,
        in_specs=[vmem] * 6,
        out_specs=vmem,
        out_shape=jax.ShapeDtypeStruct((256, LAGS), BF),
        compiler_params=pltpu.CompilerParams(vmem_limit_bytes=32 * 1024 * 1024),
        name="pairs",
    )(rim, *parts)


def on_device(raw, send_order, pair_first, pair_offset, pair_count):
    seg_count = raw.shape[0]
    groups = lax.axis_size("seg")
    blocks = lax.axis_size("chan")
    sent = whitened(raw, send_order)
    own = lax.all_to_all(sent, "chan", split_axis=0, concat_axis=0, tiled=True)
    rim = lax.ppermute(own[: REACH // 2], "chan", [(i + 1, i) for i in range(blocks - 1)])
    parts = gathered(own, pair_first, pair_offset, pair_count, 1.0 / math.sqrt(seg_count * groups * F))
    lags = pair_lags(rim, parts)
    shares = lax.all_to_all(lags.reshape(groups, 256 // groups, LAGS), "seg", 0, 0, tiled=True)
    return jnp.sum(shares.astype(F32), axis=0)


def solution(mesh):
    return jax.shard_map(
        on_device,
        mesh=mesh,
        in_specs=(P("seg", "chan", None), P("chan"), P("chan"), P("chan"), P("chan")),
        out_specs=P(("chan", "seg"), None),
        check_vma=False,
    )
```

```python
import math

import jax
import jax.numpy as jnp
import numpy as np
from jax import lax
from jax.experimental import pallas as pl
from jax.experimental.pallas import tpu as pltpu
from jax.sharding import PartitionSpec as P

L = 1536
F = 512
BAND = 32
LAGS = 256
REACH = 48
COLS = 256
STEPS = 4
BF = jnp.bfloat16
F32 = jnp.float32


BINS = (1 + np.arange(STEPS)[:, None] + STEPS * np.arange(F // STEPS)[None, :]).reshape(F)


def forward_table():
    quarter = L // 4
    phase = (np.arange(quarter)[:, None] * BINS[None, :] % L).astype(np.float32) * np.float32(2.0 * math.pi / L)
    cosines = np.cos(phase).astype(BF).reshape(quarter, STEPS, F // STEPS)
    sines = (-np.sin(phase)).astype(BF).reshape(quarter, STEPS, F // STEPS)
    return np.ascontiguousarray(np.concatenate([cosines, sines], axis=-1).transpose(1, 0, 2))


def inverse_tables(factor):
    bins = BINS
    lag_shift = np.arange(LAGS) - LAGS // 2
    phase = (bins[:, None] * lag_shift[None, :] % L).astype(np.float64) * (2.0 * math.pi / L)
    table = (np.concatenate([np.cos(phase), -np.sin(phase)], axis=0) * factor).astype(np.float32)
    high = table.astype(BF)
    return high, (table - high.astype(np.float32)).astype(BF)


def dot(a, b):
    return jnp.dot(a, b, preferred_element_type=F32)


def spread_matrix(blocks, back):
    rows = blocks * 16
    shape = (1, rows) if back else (rows, 1)
    mixed = lax.broadcasted_iota(jnp.int32, shape, 1 if back else 0)
    target = (mixed % 16) // 2 * (2 * blocks) + mixed // 16 * 2 + mixed % 2
    apart = lax.broadcasted_iota(jnp.int32, (rows, rows), 0 if back else 1)
    return (apart == target).astype(F32).astype(BF)


def split(x):
    high = x.astype(BF)
    return high, (x - high.astype(F32)).astype(BF)


def fold(normed, even, odd, first_row):
    quarter = L // 4
    x0, x1, x2, x3 = (normed[:, i * quarter : (i + 1) * quarter] for i in range(4))
    even0, even1 = x0 + x2, x1 + x3
    count = normed.shape[0]
    upper, lower = slice(first_row, first_row + count), slice(first_row + 256, first_row + 256 + count)
    for at, value in enumerate((even0 - even1, even0 + even1)):
        even[at, upper], even[at, lower] = split(value)
    for side, value in enumerate((x0 - x2, x1 - x3)):
        columns = slice(side * quarter, (side + 1) * quarter)
        odd[upper, columns], odd[lower, columns] = split(value)


def whiten_kernel(raw_hbm, order_hbm, table_hbm, out_ref, raw_ref, order_ref, table_ref, even, odd, sems):
    width = F // STEPS
    quarter = L // 4
    visit = (0, 2, 1, 3)
    raw_copies = [pltpu.make_async_copy(raw_hbm.at[s], raw_ref.at[s], sems.at[s]) for s in range(2)]
    table_copies = {
        i: pltpu.make_async_copy(table_hbm.at[i], table_ref.at[i, :quarter], sems.at[2 + i]) for i in visit
    }
    order_copy = pltpu.make_async_copy(order_hbm, order_ref, sems.at[2 + STEPS])
    for copy in (*raw_copies, *table_copies.values(), order_copy):
        copy.start()
    mix = spread_matrix(16, False)

    def bin_at(position):
        return (position % width) * STEPS + position // width + 1

    bin_row = bin_at(lax.broadcasted_iota(jnp.int32, (F, 1), 0))
    bin_line = bin_at(lax.broadcasted_iota(jnp.int32, (1, F), 1))
    near = (jnp.abs(bin_row - bin_line) <= BAND).astype(F32).astype(BF)
    count = jnp.minimum(bin_line + BAND, F) - jnp.maximum(bin_line - BAND, 1) + 1
    share = 1.0 / count.astype(F32)

    for s in range(2):
        raw_copies[s].wait()
        for r in range(0, 128, 32):
            wave = raw_ref[s, r : r + 32].astype(F32)
            mean = jnp.sum(wave * wave, axis=-1, keepdims=True) * (1.0 / L)
            normed = (wave * lax.rsqrt(mean + 1e-05)).astype(BF).astype(F32)
            fold(normed, even, odd, s * 128 + r)
    for i in (0, 2):
        table_copies[i].wait()
        cosines = table_ref[i, :quarter, :width]
        sines = table_ref[i, :quarter, width:]
        table_ref[i, quarter:, :width] = sines if i == 0 else -sines
        table_ref[i, quarter:, width:] = -cosines if i == 0 else cosines
    real, imag = {}, {}
    for i in visit:
        if i % 2:
            table_copies[i].wait()
            both = dot(even[i // 2], table_ref[i, :quarter])
        else:
            both = dot(odd[...], table_ref[i])
        spec = both[:256] + both[256:]
        real[i] = spec[:, :width]
        imag[i] = spec[:, width:]
    power = jnp.concatenate([real[i] * real[i] + imag[i] * imag[i] for i in range(STEPS)], axis=1)
    both = dot(jnp.concatenate(split(power), axis=0), near)
    smooth = both[:256] + both[256:]
    order_copy.wait()
    factor = lax.rsqrt(smooth * share + 1e-06)
    channels = lax.broadcasted_iota(jnp.int32, (128, 128), 0)
    pick = (channels == order_ref[...]).astype(F32).T.astype(BF)
    picked = []
    for s in range(2):
        rows = slice(s * 128, s * 128 + 128)
        scaled = [x[i][rows] * factor[rows, i * width : (i + 1) * width] for x in (real, imag) for i in range(STEPS)]
        picked.append(dot(pick, jnp.concatenate(scaled, axis=1).astype(BF)).astype(BF))
    for b in range(4):
        stacked = jnp.concatenate(
            [picked[s][b * 32 : b * 32 + 32, c * COLS : (c + 1) * COLS] for c in range(4) for s in range(2)], axis=0
        )
        out_ref[b * 16 : b * 16 + 16] = dot(mix, stacked).astype(BF).reshape(16, 16, COLS)


def in_hbm(x):
    return pltpu.with_memory_space_constraint(jnp.asarray(x), pltpu.HBM)


def whitened(raw, send_order):
    hbm = pl.BlockSpec(memory_space=pltpu.HBM)
    return pl.pallas_call(
        whiten_kernel,
        in_specs=[hbm] * 3,
        out_specs=pl.BlockSpec(memory_space=pltpu.VMEM),
        out_shape=jax.ShapeDtypeStruct((64, 16, COLS), BF),
        scratch_shapes=[
            pltpu.VMEM((2, 128, L), BF),
            pltpu.VMEM((1, 128), jnp.int32),
            pltpu.VMEM((STEPS, L // 2, COLS), BF),
            pltpu.VMEM((2, 512, L // 4), BF),
            pltpu.VMEM((512, L // 2), BF),
            pltpu.SemaphoreType.DMA((3 + STEPS,)),
        ],
        compiler_params=pltpu.CompilerParams(vmem_limit_bytes=32 * 1024 * 1024),
        name="whiten",
    )(*(in_hbm(x) for x in (raw, send_order.reshape(1, 128), forward_table())))


def gather_kernel(
    own_ref, count_ref, first_hbm, offset_hbm, high_hbm, low_hbm,
    left_ref, right_ref, pick_ref, high_ref, low_ref,
    rows_ref, first_ref, offset_ref, sems,
):
    moves = ((first_hbm, first_ref), (offset_hbm, offset_ref), (high_hbm, high_ref), (low_hbm, low_ref))
    copies = [pltpu.make_async_copy(src, dst, sems.at[i]) for i, (src, dst) in enumerate(moves)]
    for copy in copies:
        copy.start()
    apart = spread_matrix(16, True)
    for b in range(4):
        block = dot(apart, own_ref[b * 16 : b * 16 + 16].reshape(256, COLS)).astype(BF)
        for c in range(4):
            for s in range(2):
                at = (c * 2 + s) * 32
                rows_ref[s, c, b * 32 : b * 32 + 32] = block[at : at + 32]
    for copy in copies[:2]:
        copy.wait()
    first = first_ref[...]
    second = first + offset_ref[...]
    slot = lax.broadcasted_iota(jnp.int32, (1, 256), 1)
    live_first = jnp.where(slot < count_ref[0], first, -1)
    at = lax.broadcasted_iota(jnp.int32, (128, 256), 0)
    left_pick = (at == live_first).astype(F32).T.astype(BF)
    right_pick = (at == second).astype(F32).T.astype(BF)
    pick_ref[...] = (at + 128 == second).astype(F32).T.astype(BF)
    for s in range(2):
        for c in range(4):
            rows = rows_ref[s, c]
            left_ref[s, c] = dot(left_pick, rows).astype(BF)
            right_ref[s, c] = dot(right_pick, rows).astype(BF)
    for copy in copies[2:]:
        copy.wait()


def gathered(own, pair_first, pair_offset, pair_count, factor):
    high, low = inverse_tables(factor)
    vmem = pl.BlockSpec(memory_space=pltpu.VMEM)
    hbm = pl.BlockSpec(memory_space=pltpu.HBM)
    rows = jax.ShapeDtypeStruct((2, 4, 256, COLS), BF)
    table = jax.ShapeDtypeStruct((2 * F, LAGS), BF)
    return pl.pallas_call(
        gather_kernel,
        in_specs=[vmem, pl.BlockSpec(memory_space=pltpu.SMEM)] + [hbm] * 4,
        out_specs=[vmem] * 5,
        out_shape=[rows, rows, jax.ShapeDtypeStruct((256, 128), BF), table, table],
        scratch_shapes=[
            pltpu.VMEM((2, 4, 128, COLS), BF),
            pltpu.VMEM((1, 256), jnp.int32),
            pltpu.VMEM((1, 256), jnp.int32),
            pltpu.SemaphoreType.DMA((4,)),
        ],
        compiler_params=pltpu.CompilerParams(vmem_limit_bytes=32 * 1024 * 1024),
        name="gather",
    )(own, pair_count, *(in_hbm(x) for x in (pair_first.reshape(1, 256), pair_offset.reshape(1, 256), high, low)))


def pairs_kernel(rim_ref, left_ref, right_ref, pick_ref, high_ref, low_ref, out_ref, rim_rows, parts_ref):
    apart = spread_matrix(8, True)
    for b in range(3):
        block = dot(apart, rim_ref[b * 8 : b * 8 + 8].reshape(128, COLS)).astype(BF)
        for c in range(4):
            for s in range(2):
                at = (c * 2 + s) * 16
                rim_rows[s, c, b * 16 : b * 16 + 16] = block[at : at + 16]
    pick = pick_ref[:, :REACH]

    def right(s, c):
        return right_ref[s, c].astype(F32) + dot(pick, rim_rows[s, c])

    for c in range(2):
        re = im = None
        for s in range(2):
            a_re, a_im = left_ref[s, c].astype(F32), left_ref[s, c + 2].astype(F32)
            c_re, c_im = right(s, c), right(s, c + 2)
            one, two = a_re * c_re + a_im * c_im, a_im * c_re - a_re * c_im
            re = one if re is None else re + one
            im = two if im is None else im + two
        for part, at in ((re, c * COLS), (im, (c + 2) * COLS)):
            parts_ref[:256, at : at + COLS], parts_ref[256:, at : at + COLS] = split(part)
    both = dot(parts_ref[...], high_ref[...])
    total = both[:256] + both[256:] + dot(parts_ref[:256], low_ref[...])
    out_ref[...] = total.astype(BF)


def pair_lags(rim, parts):
    vmem = pl.BlockSpec(memory_space=pltpu.VMEM)
    return pl.pallas_call(
        pairs_kernel,
        in_specs=[vmem] * 6,
        out_specs=vmem,
        out_shape=jax.ShapeDtypeStruct((256, LAGS), BF),
        scratch_shapes=[pltpu.VMEM((2, 4, REACH, COLS), BF), pltpu.VMEM((512, 2 * F), BF)],
        compiler_params=pltpu.CompilerParams(vmem_limit_bytes=32 * 1024 * 1024),
        name="pairs",
    )(rim, *parts)


def on_device(raw, send_order, pair_first, pair_offset, pair_count):
    seg_count = raw.shape[0]
    groups = lax.axis_size("seg")
    blocks = lax.axis_size("chan")
    sent = whitened(raw, send_order)
    own = lax.all_to_all(sent, "chan", split_axis=0, concat_axis=0, tiled=True)
    rim = lax.ppermute(own[: REACH // 2], "chan", [(i + 1, i) for i in range(blocks - 1)])
    parts = gathered(own, pair_first, pair_offset, pair_count, 1.0 / math.sqrt(seg_count * groups * F))
    lags = pair_lags(rim, parts)
    shares = lax.all_to_all(lags.reshape(groups, 256 // groups, LAGS), "seg", 0, 0, tiled=True)
    return jnp.sum(shares.astype(F32), axis=0)


def solution(mesh):
    return jax.shard_map(
        on_device,
        mesh=mesh,
        in_specs=(P("seg", "chan", None), P("chan"), P("chan"), P("chan"), P("chan")),
        out_specs=P(("chan", "seg"), None),
        check_vma=False,
    )
```

```python
import math

import jax
import jax.numpy as jnp
import numpy as np
from jax import lax
from jax.experimental import pallas as pl
from jax.experimental.pallas import tpu as pltpu
from jax.sharding import PartitionSpec as P

L = 1536
F = 512
BAND = 32
LAGS = 256
REACH = 48
COLS = 256
STEPS = 4
BF = jnp.bfloat16
F32 = jnp.float32


BINS = (1 + np.arange(STEPS)[:, None] + STEPS * np.arange(F // STEPS)[None, :]).reshape(F)


def forward_table():
    quarter = L // 4
    phase = (np.arange(quarter)[:, None] * BINS[None, :] % L).astype(np.float32) * np.float32(2.0 * math.pi / L)
    cosines = np.cos(phase).astype(BF).reshape(quarter, STEPS, F // STEPS)
    sines = (-np.sin(phase)).astype(BF).reshape(quarter, STEPS, F // STEPS)
    return np.concatenate([cosines, sines], axis=-1)[:, (0, 2, 1, 3)].reshape(quarter, 2 * F)


def inverse_tables(factor):
    bins = BINS
    lag_shift = np.arange(LAGS) - LAGS // 2
    phase = (bins[:, None] * lag_shift[None, :] % L).astype(np.float64) * (2.0 * math.pi / L)
    table = (np.concatenate([np.cos(phase), -np.sin(phase)], axis=0) * factor).astype(np.float32)
    high = table.astype(BF)
    return high, (table - high.astype(np.float32)).astype(BF)


def dot(a, b):
    return jnp.dot(a, b, preferred_element_type=F32)


def spread_matrix(blocks, back):
    rows = blocks * 16
    shape = (1, rows) if back else (rows, 1)
    mixed = lax.broadcasted_iota(jnp.int32, shape, 1 if back else 0)
    target = (mixed % 16) // 2 * (2 * blocks) + mixed // 16 * 2 + mixed % 2
    apart = lax.broadcasted_iota(jnp.int32, (rows, rows), 0 if back else 1)
    return (apart == target).astype(F32).astype(BF)


def split(x):
    high = x.astype(BF)
    return high, (x - high.astype(F32)).astype(BF)


def fold(normed, even, odd, first_row):
    quarter = L // 4
    x0, x1, x2, x3 = (normed[:, i * quarter : (i + 1) * quarter] for i in range(4))
    even0, even1 = x0 + x2, x1 + x3
    count = normed.shape[0]
    upper, lower = slice(first_row, first_row + count), slice(first_row + 256, first_row + 256 + count)
    for at, value in enumerate((even0 - even1, even0 + even1)):
        even[at, upper], even[at, lower] = split(value)
    for side, value in enumerate((x0 - x2, x1 - x3)):
        columns = slice(side * quarter, (side + 1) * quarter)
        odd[upper, columns], odd[lower, columns] = split(value)


def whiten_kernel(raw_hbm, order_hbm, table_hbm, out_ref, raw_ref, order_ref, table_ref, even, odd, sems):
    width = F // STEPS
    quarter = L // 4
    raw_copy = pltpu.make_async_copy(raw_hbm, raw_ref, sems.at[0])
    table_copy = pltpu.make_async_copy(table_hbm, table_ref.at[:quarter], sems.at[1])
    order_copy = pltpu.make_async_copy(order_hbm, order_ref, sems.at[2])
    for copy in (raw_copy, table_copy, order_copy):
        copy.start()
    mix = spread_matrix(16, False)

    def bin_at(position):
        return (position % width) * STEPS + position // width + 1

    bin_row = bin_at(lax.broadcasted_iota(jnp.int32, (F, 1), 0))
    bin_line = bin_at(lax.broadcasted_iota(jnp.int32, (1, F), 1))
    near = (jnp.abs(bin_row - bin_line) <= BAND).astype(F32).astype(BF)
    count = jnp.minimum(bin_line + BAND, F) - jnp.maximum(bin_line - BAND, 1) + 1
    share = 1.0 / count.astype(F32)

    raw_copy.wait()
    for s in range(2):
        for r in range(0, 128, 16):
            wave = raw_ref[s, r : r + 16].astype(F32)
            mean = jnp.sum(wave * wave, axis=-1, keepdims=True) * (1.0 / L)
            normed = (wave * lax.rsqrt(mean + 1e-05)).astype(BF).astype(F32)
            fold(normed, even, odd, s * 128 + r)
    table_copy.wait()
    specs = {}
    for i in (1, 3):
        at = 2 * COLS + (i // 2) * COLS
        both = dot(even[i // 2], table_ref[:quarter, at : at + COLS])
        specs[i] = both[:256] + both[256:]
    for at in (0, COLS):
        cosines = table_ref[:quarter, at : at + width]
        sines = table_ref[:quarter, at + width : at + COLS]
        table_ref[quarter:, at : at + width] = sines if at == 0 else -sines
        table_ref[quarter:, at + width : at + COLS] = -cosines if at == 0 else cosines
    both = dot(odd[...], table_ref[:, : 2 * COLS])
    for i in (0, 2):
        at = (i // 2) * COLS
        specs[i] = both[:256, at : at + COLS] + both[256:, at : at + COLS]
    real, imag = {}, {}
    for i, spec in specs.items():
        real[i] = spec[:, :width]
        imag[i] = spec[:, width:]
    power = jnp.concatenate([real[i] * real[i] + imag[i] * imag[i] for i in range(STEPS)], axis=1)
    smooth = dot(power.astype(BF), near)
    order_copy.wait()
    factor = lax.rsqrt(smooth * share + 1e-06)
    channels = lax.broadcasted_iota(jnp.int32, (128, 128), 0)
    pick = (channels == order_ref[...]).astype(F32).T.astype(BF)
    picked = []
    for s in range(2):
        rows = slice(s * 128, s * 128 + 128)
        scaled = [x[i][rows] * factor[rows, i * width : (i + 1) * width] for x in (real, imag) for i in range(STEPS)]
        picked.append(dot(pick, jnp.concatenate(scaled, axis=1).astype(BF)).astype(BF))
    for b in range(4):
        stacked = jnp.concatenate(
            [picked[s][b * 32 : b * 32 + 32, c * COLS : (c + 1) * COLS] for c in range(4) for s in range(2)], axis=0
        )
        out_ref[b * 16 : b * 16 + 16] = dot(mix, stacked).astype(BF).reshape(16, 16, COLS)


def in_hbm(x):
    return pltpu.with_memory_space_constraint(jnp.asarray(x), pltpu.HBM)


def whitened(raw, send_order):
    hbm = pl.BlockSpec(memory_space=pltpu.HBM)
    return pl.pallas_call(
        whiten_kernel,
        in_specs=[hbm] * 3,
        out_specs=pl.BlockSpec(memory_space=pltpu.VMEM),
        out_shape=jax.ShapeDtypeStruct((64, 16, COLS), BF),
        scratch_shapes=[
            pltpu.VMEM((2, 128, L), BF),
            pltpu.VMEM((1, 128), jnp.int32),
            pltpu.VMEM((L // 2, 2 * F), BF),
            pltpu.VMEM((2, 512, L // 4), BF),
            pltpu.VMEM((512, L // 2), BF),
            pltpu.SemaphoreType.DMA((3,)),
        ],
        compiler_params=pltpu.CompilerParams(vmem_limit_bytes=32 * 1024 * 1024),
        name="whiten",
    )(*(in_hbm(x) for x in (raw, send_order.reshape(1, 128), forward_table())))


def gather_kernel(
    own_ref, count_ref, first_hbm, offset_hbm, high_hbm, low_hbm,
    left_ref, right_ref, pick_ref, high_ref, low_ref,
    rows_ref, first_ref, offset_ref, sems,
):
    moves = ((first_hbm, first_ref), (offset_hbm, offset_ref), (high_hbm, high_ref), (low_hbm, low_ref))
    copies = [pltpu.make_async_copy(src, dst, sems.at[i]) for i, (src, dst) in enumerate(moves)]
    for copy in copies:
        copy.start()
    apart = spread_matrix(16, True)
    for b in range(4):
        block = dot(apart, own_ref[b * 16 : b * 16 + 16].reshape(256, COLS)).astype(BF)
        for c in range(4):
            for s in range(2):
                at = (c * 2 + s) * 32
                rows_ref[s, c, b * 32 : b * 32 + 32] = block[at : at + 32]
    for copy in copies[:2]:
        copy.wait()
    first = first_ref[...]
    second = first + offset_ref[...]
    slot = lax.broadcasted_iota(jnp.int32, (1, 256), 1)
    live_first = jnp.where(slot < count_ref[0], first, -1)
    at = lax.broadcasted_iota(jnp.int32, (128, 256), 0)
    left_pick = (at == live_first).astype(F32).T.astype(BF)
    right_pick = (at == second).astype(F32).T.astype(BF)
    pick_ref[...] = (at + 128 == second).astype(F32).T.astype(BF)
    for s in range(2):
        for c in range(4):
            rows = rows_ref[s, c]
            left_ref[s, c] = dot(left_pick, rows).astype(BF)
            right_ref[s, c] = dot(right_pick, rows).astype(BF)
    for copy in copies[2:]:
        copy.wait()


def gathered(own, pair_first, pair_offset, pair_count, factor):
    high, low = inverse_tables(factor)
    vmem = pl.BlockSpec(memory_space=pltpu.VMEM)
    hbm = pl.BlockSpec(memory_space=pltpu.HBM)
    rows = jax.ShapeDtypeStruct((2, 4, 256, COLS), BF)
    table = jax.ShapeDtypeStruct((2 * F, LAGS), BF)
    return pl.pallas_call(
        gather_kernel,
        in_specs=[vmem, pl.BlockSpec(memory_space=pltpu.SMEM)] + [hbm] * 4,
        out_specs=[vmem] * 5,
        out_shape=[rows, rows, jax.ShapeDtypeStruct((256, 128), BF), table, table],
        scratch_shapes=[
            pltpu.VMEM((2, 4, 128, COLS), BF),
            pltpu.VMEM((1, 256), jnp.int32),
            pltpu.VMEM((1, 256), jnp.int32),
            pltpu.SemaphoreType.DMA((4,)),
        ],
        compiler_params=pltpu.CompilerParams(vmem_limit_bytes=32 * 1024 * 1024),
        name="gather",
    )(own, pair_count, *(in_hbm(x) for x in (pair_first.reshape(1, 256), pair_offset.reshape(1, 256), high, low)))


def pairs_kernel(rim_ref, left_ref, right_ref, pick_ref, high_ref, low_ref, out_ref, rim_rows, parts_ref):
    apart = spread_matrix(8, True)
    for b in range(3):
        block = dot(apart, rim_ref[b * 8 : b * 8 + 8].reshape(128, COLS)).astype(BF)
        for c in range(4):
            for s in range(2):
                at = (c * 2 + s) * 16
                rim_rows[s, c, b * 16 : b * 16 + 16] = block[at : at + 16]
    pick = pick_ref[:, :REACH]

    def right(s, c):
        return right_ref[s, c].astype(F32) + dot(pick, rim_rows[s, c])

    for c in range(2):
        re = im = None
        for s in range(2):
            a_re, a_im = left_ref[s, c].astype(F32), left_ref[s, c + 2].astype(F32)
            c_re, c_im = right(s, c), right(s, c + 2)
            one, two = a_re * c_re + a_im * c_im, a_im * c_re - a_re * c_im
            re = one if re is None else re + one
            im = two if im is None else im + two
        for part, at in ((re, c * COLS), (im, (c + 2) * COLS)):
            parts_ref[:256, at : at + COLS], parts_ref[256:, at : at + COLS] = split(part)
    both = dot(parts_ref[...], high_ref[...])
    total = both[:256] + both[256:] + dot(parts_ref[:256], low_ref[...])
    out_ref[...] = total.astype(BF)


def pair_lags(rim, parts):
    vmem = pl.BlockSpec(memory_space=pltpu.VMEM)
    return pl.pallas_call(
        pairs_kernel,
        in_specs=[vmem] * 6,
        out_specs=vmem,
        out_shape=jax.ShapeDtypeStruct((256, LAGS), BF),
        scratch_shapes=[pltpu.VMEM((2, 4, REACH, COLS), BF), pltpu.VMEM((512, 2 * F), BF)],
        compiler_params=pltpu.CompilerParams(vmem_limit_bytes=32 * 1024 * 1024),
        name="pairs",
    )(rim, *parts)


def on_device(raw, send_order, pair_first, pair_offset, pair_count):
    seg_count = raw.shape[0]
    groups = lax.axis_size("seg")
    blocks = lax.axis_size("chan")
    sent = whitened(raw, send_order)
    own = lax.all_to_all(sent, "chan", split_axis=0, concat_axis=0, tiled=True)
    rim = lax.ppermute(own[: REACH // 2], "chan", [(i + 1, i) for i in range(blocks - 1)])
    parts = gathered(own, pair_first, pair_offset, pair_count, 1.0 / math.sqrt(seg_count * groups * F))
    lags = pair_lags(rim, parts)
    shares = lax.all_to_all(lags.reshape(groups, 256 // groups, LAGS), "seg", 0, 0, tiled=True)
    return jnp.sum(shares.astype(F32), axis=0)


def solution(mesh):
    return jax.shard_map(
        on_device,
        mesh=mesh,
        in_specs=(P("seg", "chan", None), P("chan"), P("chan"), P("chan"), P("chan")),
        out_specs=P(("chan", "seg"), None),
        check_vma=False,
    )
```

```python
import math

import jax
import jax.numpy as jnp
import numpy as np
from jax import lax
from jax.experimental import pallas as pl
from jax.experimental.pallas import tpu as pltpu
from jax.sharding import PartitionSpec as P

L = 1536
F = 512
BAND = 32
LAGS = 256
REACH = 48
COLS = 256
STEPS = 4
BF = jnp.bfloat16
F32 = jnp.float32


BINS = (1 + np.arange(STEPS)[:, None] + STEPS * np.arange(F // STEPS)[None, :]).reshape(F)


def forward_table():
    quarter = L // 4
    phase = (np.arange(quarter)[:, None] * BINS[None, :] % L).astype(np.float32) * np.float32(2.0 * math.pi / L)
    cosines = np.cos(phase).astype(BF).reshape(quarter, STEPS, F // STEPS)
    sines = (-np.sin(phase)).astype(BF).reshape(quarter, STEPS, F // STEPS)
    return np.concatenate([cosines, sines], axis=-1)[:, (0, 2, 1, 3)].reshape(quarter, 2 * F)


def inverse_tables(factor):
    bins = BINS
    lag_shift = np.arange(LAGS) - LAGS // 2
    phase = (bins[:, None] * lag_shift[None, :] % L).astype(np.float64) * (2.0 * math.pi / L)
    table = (np.concatenate([np.cos(phase), -np.sin(phase)], axis=0) * factor).astype(np.float32)
    high = table.astype(BF)
    return high, (table - high.astype(np.float32)).astype(BF)


def dot(a, b):
    return jnp.dot(a, b, preferred_element_type=F32)


def spread_matrix(blocks, back):
    rows = blocks * 16
    shape = (1, rows) if back else (rows, 1)
    mixed = lax.broadcasted_iota(jnp.int32, shape, 1 if back else 0)
    target = (mixed % 16) // 2 * (2 * blocks) + mixed // 16 * 2 + mixed % 2
    apart = lax.broadcasted_iota(jnp.int32, (rows, rows), 0 if back else 1)
    return (apart == target).astype(F32).astype(BF)


def split(x):
    high = x.astype(BF)
    return high, (x - high.astype(F32)).astype(BF)


def fold(normed, even, odd, first_row):
    quarter = L // 4
    x0, x1, x2, x3 = (normed[:, i * quarter : (i + 1) * quarter] for i in range(4))
    even0, even1 = x0 + x2, x1 + x3
    count = normed.shape[0]
    upper, lower = slice(first_row, first_row + count), slice(first_row + 256, first_row + 256 + count)
    for at, value in enumerate((even0 - even1, even0 + even1)):
        even[at, upper], even[at, lower] = split(value)
    for side, value in enumerate((x0 - x2, x1 - x3)):
        columns = slice(side * quarter, (side + 1) * quarter)
        odd[upper, columns], odd[lower, columns] = split(value)


def whiten_kernel(raw_hbm, order_hbm, table_hbm, out_ref, raw_ref, order_ref, table_ref, even, odd, sems):
    width = F // STEPS
    quarter = L // 4
    raw_copy = pltpu.make_async_copy(raw_hbm, raw_ref, sems.at[0])
    table_copy = pltpu.make_async_copy(table_hbm, table_ref.at[:quarter], sems.at[1])
    order_copy = pltpu.make_async_copy(order_hbm, order_ref, sems.at[2])
    for copy in (order_copy, raw_copy, table_copy):
        copy.start()
    mix = spread_matrix(16, False)

    def bin_at(position):
        return (position % width) * STEPS + position // width + 1

    bin_row = bin_at(lax.broadcasted_iota(jnp.int32, (F, 1), 0))
    bin_line = bin_at(lax.broadcasted_iota(jnp.int32, (1, F), 1))
    near = (jnp.abs(bin_row - bin_line) <= BAND).astype(F32).astype(BF)
    count = jnp.minimum(bin_line + BAND, F) - jnp.maximum(bin_line - BAND, 1) + 1
    share = 1.0 / count.astype(F32)

    order_copy.wait()
    channels = lax.broadcasted_iota(jnp.int32, (128, 128), 0)
    pick = (channels == order_ref[...]).astype(F32).T.astype(BF)
    raw_copy.wait()
    table_copy.wait()
    for s in range(2):
        for r in range(0, 128, 16):
            wave = raw_ref[s, r : r + 16].astype(F32)
            mean = jnp.sum(wave * wave, axis=-1, keepdims=True) * (1.0 / L)
            normed = (wave * lax.rsqrt(mean + 1e-05)).astype(BF).astype(F32)
            fold(normed, even, odd, s * 128 + r)
    specs = {}
    for i in (1, 3):
        at = 2 * COLS + (i // 2) * COLS
        both = dot(even[i // 2], table_ref[:quarter, at : at + COLS])
        specs[i] = both[:256] + both[256:]
    for at in (0, COLS):
        cosines = table_ref[:quarter, at : at + width]
        sines = table_ref[:quarter, at + width : at + COLS]
        table_ref[quarter:, at : at + width] = sines if at == 0 else -sines
        table_ref[quarter:, at + width : at + COLS] = -cosines if at == 0 else cosines
    both = dot(odd[...], table_ref[:, : 2 * COLS])
    for i in (0, 2):
        at = (i // 2) * COLS
        specs[i] = both[:256, at : at + COLS] + both[256:, at : at + COLS]
    real, imag = {}, {}
    for i, spec in specs.items():
        real[i] = spec[:, :width]
        imag[i] = spec[:, width:]
    power = jnp.concatenate([real[i] * real[i] + imag[i] * imag[i] for i in range(STEPS)], axis=1)
    smooth = dot(power.astype(BF), near)
    factor = lax.rsqrt(smooth * share + 1e-06)
    picked = []
    for s in range(2):
        rows = slice(s * 128, s * 128 + 128)
        scaled = [x[i][rows] * factor[rows, i * width : (i + 1) * width] for x in (real, imag) for i in range(STEPS)]
        picked.append(dot(pick, jnp.concatenate(scaled, axis=1).astype(BF)).astype(BF))
    for b in range(4):
        stacked = jnp.concatenate(
            [picked[s][b * 32 : b * 32 + 32, c * COLS : (c + 1) * COLS] for c in range(4) for s in range(2)], axis=0
        )
        out_ref[b * 16 : b * 16 + 16] = dot(mix, stacked).astype(BF).reshape(16, 16, COLS)


def in_hbm(x):
    return pltpu.with_memory_space_constraint(jnp.asarray(x), pltpu.HBM)


def whitened(raw, send_order):
    hbm = pl.BlockSpec(memory_space=pltpu.HBM)
    return pl.pallas_call(
        whiten_kernel,
        in_specs=[hbm] * 3,
        out_specs=pl.BlockSpec(memory_space=pltpu.VMEM),
        out_shape=jax.ShapeDtypeStruct((64, 16, COLS), BF),
        scratch_shapes=[
            pltpu.VMEM((2, 128, L), BF),
            pltpu.VMEM((1, 128), jnp.int32),
            pltpu.VMEM((L // 2, 2 * F), BF),
            pltpu.VMEM((2, 512, L // 4), BF),
            pltpu.VMEM((512, L // 2), BF),
            pltpu.SemaphoreType.DMA((3,)),
        ],
        compiler_params=pltpu.CompilerParams(vmem_limit_bytes=32 * 1024 * 1024),
        name="whiten",
    )(*(in_hbm(x) for x in (raw, send_order.reshape(1, 128), forward_table())))


def gather_kernel(
    own_ref, count_ref, first_hbm, offset_hbm, high_hbm, low_hbm,
    left_ref, right_ref, pick_ref, high_ref, low_ref,
    rows_ref, first_ref, offset_ref, sems,
):
    moves = ((first_hbm, first_ref), (offset_hbm, offset_ref), (high_hbm, high_ref), (low_hbm, low_ref))
    copies = [pltpu.make_async_copy(src, dst, sems.at[i]) for i, (src, dst) in enumerate(moves)]
    for copy in copies:
        copy.start()
    apart = spread_matrix(16, True)
    for b in range(4):
        block = dot(apart, own_ref[b * 16 : b * 16 + 16].reshape(256, COLS)).astype(BF)
        for c in range(4):
            for s in range(2):
                at = (c * 2 + s) * 32
                rows_ref[s, c, b * 32 : b * 32 + 32] = block[at : at + 32]
    for copy in copies[:2]:
        copy.wait()
    first = first_ref[...]
    second = first + offset_ref[...]
    slot = lax.broadcasted_iota(jnp.int32, (1, 256), 1)
    live_first = jnp.where(slot < count_ref[0], first, -1)
    at = lax.broadcasted_iota(jnp.int32, (128, 256), 0)
    left_pick = (at == live_first).astype(F32).T.astype(BF)
    right_pick = (at == second).astype(F32).T.astype(BF)
    pick_ref[...] = (at + 128 == second).astype(F32).T.astype(BF)
    for s in range(2):
        for c in range(4):
            rows = rows_ref[s, c]
            left_ref[s, c] = dot(left_pick, rows).astype(BF)
            right_ref[s, c] = dot(right_pick, rows).astype(BF)
    for copy in copies[2:]:
        copy.wait()


def gathered(own, pair_first, pair_offset, pair_count, factor):
    high, low = inverse_tables(factor)
    vmem = pl.BlockSpec(memory_space=pltpu.VMEM)
    hbm = pl.BlockSpec(memory_space=pltpu.HBM)
    rows = jax.ShapeDtypeStruct((2, 4, 256, COLS), BF)
    table = jax.ShapeDtypeStruct((2 * F, LAGS), BF)
    return pl.pallas_call(
        gather_kernel,
        in_specs=[vmem, pl.BlockSpec(memory_space=pltpu.SMEM)] + [hbm] * 4,
        out_specs=[vmem] * 5,
        out_shape=[rows, rows, jax.ShapeDtypeStruct((256, 128), BF), table, table],
        scratch_shapes=[
            pltpu.VMEM((2, 4, 128, COLS), BF),
            pltpu.VMEM((1, 256), jnp.int32),
            pltpu.VMEM((1, 256), jnp.int32),
            pltpu.SemaphoreType.DMA((4,)),
        ],
        compiler_params=pltpu.CompilerParams(vmem_limit_bytes=32 * 1024 * 1024),
        name="gather",
    )(own, pair_count, *(in_hbm(x) for x in (pair_first.reshape(1, 256), pair_offset.reshape(1, 256), high, low)))


def pairs_kernel(rim_ref, left_ref, right_ref, pick_ref, high_ref, low_ref, out_ref, rim_rows, parts_ref):
    apart = spread_matrix(8, True)
    for b in range(3):
        block = dot(apart, rim_ref[b * 8 : b * 8 + 8].reshape(128, COLS)).astype(BF)
        for c in range(4):
            for s in range(2):
                at = (c * 2 + s) * 16
                rim_rows[s, c, b * 16 : b * 16 + 16] = block[at : at + 16]
    pick = pick_ref[:, :REACH]

    def right(s, c):
        return right_ref[s, c].astype(F32) + dot(pick, rim_rows[s, c])

    for c in range(2):
        re = im = None
        for s in range(2):
            a_re, a_im = left_ref[s, c].astype(F32), left_ref[s, c + 2].astype(F32)
            c_re, c_im = right(s, c), right(s, c + 2)
            one, two = a_re * c_re + a_im * c_im, a_im * c_re - a_re * c_im
            re = one if re is None else re + one
            im = two if im is None else im + two
        for part, at in ((re, c * COLS), (im, (c + 2) * COLS)):
            parts_ref[:256, at : at + COLS], parts_ref[256:, at : at + COLS] = split(part)
    both = dot(parts_ref[...], high_ref[...])
    total = both[:256] + both[256:] + dot(parts_ref[:256], low_ref[...])
    out_ref[...] = total.astype(BF)


def pair_lags(rim, parts):
    vmem = pl.BlockSpec(memory_space=pltpu.VMEM)
    return pl.pallas_call(
        pairs_kernel,
        in_specs=[vmem] * 6,
        out_specs=vmem,
        out_shape=jax.ShapeDtypeStruct((256, LAGS), BF),
        scratch_shapes=[pltpu.VMEM((2, 4, REACH, COLS), BF), pltpu.VMEM((512, 2 * F), BF)],
        compiler_params=pltpu.CompilerParams(vmem_limit_bytes=32 * 1024 * 1024),
        name="pairs",
    )(rim, *parts)


def on_device(raw, send_order, pair_first, pair_offset, pair_count):
    seg_count = raw.shape[0]
    groups = lax.axis_size("seg")
    blocks = lax.axis_size("chan")
    sent = whitened(raw, send_order)
    own = lax.all_to_all(sent, "chan", split_axis=0, concat_axis=0, tiled=True)
    rim = lax.ppermute(own[: REACH // 2], "chan", [(i + 1, i) for i in range(blocks - 1)])
    parts = gathered(own, pair_first, pair_offset, pair_count, 1.0 / math.sqrt(seg_count * groups * F))
    lags = pair_lags(rim, parts)
    shares = lax.all_to_all(lags.reshape(groups, 256 // groups, LAGS), "seg", 0, 0, tiled=True)
    return jnp.sum(shares.astype(F32), axis=0)


def solution(mesh):
    return jax.shard_map(
        on_device,
        mesh=mesh,
        in_specs=(P("seg", "chan", None), P("chan"), P("chan"), P("chan"), P("chan")),
        out_specs=P(("chan", "seg"), None),
        check_vma=False,
    )
```

```python
import math

import jax
import jax.numpy as jnp
import numpy as np
from jax import lax
from jax.experimental import pallas as pl
from jax.experimental.pallas import tpu as pltpu
from jax.sharding import PartitionSpec as P

L = 1536
F = 512
BAND = 32
LAGS = 256
REACH = 48
COLS = 256
STEPS = 4
BF = jnp.bfloat16
F32 = jnp.float32


BINS = (1 + np.arange(STEPS)[:, None] + STEPS * np.arange(F // STEPS)[None, :]).reshape(F)


def forward_table():
    quarter = L // 4
    phase = (np.arange(quarter)[:, None] * BINS[None, :] % L).astype(np.float32) * np.float32(2.0 * math.pi / L)
    cosines = np.cos(phase).astype(BF).reshape(quarter, STEPS, F // STEPS)
    sines = (-np.sin(phase)).astype(BF).reshape(quarter, STEPS, F // STEPS)
    return np.concatenate([cosines, sines], axis=-1)[:, (0, 2, 1, 3)].reshape(quarter, 2 * F)


def inverse_tables(factor):
    bins = BINS
    lag_shift = np.arange(LAGS) - LAGS // 2
    phase = (bins[:, None] * lag_shift[None, :] % L).astype(np.float64) * (2.0 * math.pi / L)
    table = (np.concatenate([np.cos(phase), -np.sin(phase)], axis=0) * factor).astype(np.float32)
    high = table.astype(BF)
    return high, (table - high.astype(np.float32)).astype(BF)


def dot(a, b):
    return jnp.dot(a, b, preferred_element_type=F32)


def spread_matrix(blocks, back):
    rows = blocks * 16
    shape = (1, rows) if back else (rows, 1)
    mixed = lax.broadcasted_iota(jnp.int32, shape, 1 if back else 0)
    target = (mixed % 16) // 2 * (2 * blocks) + mixed // 16 * 2 + mixed % 2
    apart = lax.broadcasted_iota(jnp.int32, (rows, rows), 0 if back else 1)
    return (apart == target).astype(F32).astype(BF)


def split(x):
    high = x.astype(BF)
    return high, (x - high.astype(F32)).astype(BF)


def fold(normed, even, odd, first_row):
    quarter = L // 4
    x0, x1, x2, x3 = (normed[:, i * quarter : (i + 1) * quarter] for i in range(4))
    even0, even1 = x0 + x2, x1 + x3
    count = normed.shape[0]
    upper, lower = slice(first_row, first_row + count), slice(first_row + 256, first_row + 256 + count)
    for at, value in enumerate((even0 - even1, even0 + even1)):
        even[at, upper, :quarter], even[at, upper, quarter:] = split(value)
    for side, value in enumerate((x0 - x2, x1 - x3)):
        columns = slice(side * quarter, (side + 1) * quarter)
        odd[upper, columns], odd[lower, columns] = split(value)


def whiten_kernel(raw_hbm, order_hbm, table_hbm, out_ref, raw_ref, order_ref, table_ref, even, odd, sems):
    width = F // STEPS
    quarter = L // 4
    raw_copies = [pltpu.make_async_copy(raw_hbm.at[s], raw_ref.at[s], sems.at[3 * s]) for s in range(2)]
    table_copy = pltpu.make_async_copy(table_hbm, table_ref.at[:quarter], sems.at[1])
    order_copy = pltpu.make_async_copy(order_hbm, order_ref, sems.at[2])
    for copy in (order_copy, *raw_copies, table_copy):
        copy.start()
    mix = spread_matrix(16, False)

    def bin_at(position):
        return (position % width) * STEPS + position // width + 1

    bin_row = bin_at(lax.broadcasted_iota(jnp.int32, (F, 1), 0))
    bin_line = bin_at(lax.broadcasted_iota(jnp.int32, (1, F), 1))
    near = (jnp.abs(bin_row - bin_line) <= BAND).astype(F32).astype(BF)
    count = jnp.minimum(bin_line + BAND, F) - jnp.maximum(bin_line - BAND, 1) + 1
    share = 1.0 / count.astype(F32)

    order_copy.wait()
    channels = lax.broadcasted_iota(jnp.int32, (128, 128), 0)
    pick = (channels == order_ref[...]).astype(F32).T.astype(BF)
    for s in range(2):
        raw_copies[s].wait()
        if s == 1:
            table_copy.wait()
        for r in range(0, 128, 16):
            wave = raw_ref[s, r : r + 16].astype(F32)
            mean = jnp.sum(wave * wave, axis=-1, keepdims=True) * (1.0 / L)
            normed = (wave * lax.rsqrt(mean + 1e-05)).astype(BF).astype(F32)
            fold(normed, even, odd, s * 128 + r)
    specs = {}
    for i in (1, 3):
        at = 2 * COLS + (i // 2) * COLS
        table_ref[quarter:, at : at + COLS] = table_ref[:quarter, at : at + COLS]
        specs[i] = dot(even[i // 2], table_ref[:, at : at + COLS])
    for at in (0, COLS):
        cosines = table_ref[:quarter, at : at + width]
        sines = table_ref[:quarter, at + width : at + COLS]
        table_ref[quarter:, at : at + width] = sines if at == 0 else -sines
        table_ref[quarter:, at + width : at + COLS] = -cosines if at == 0 else cosines
    both = dot(odd[...], table_ref[:, : 2 * COLS])
    for i in (0, 2):
        at = (i // 2) * COLS
        specs[i] = both[:256, at : at + COLS] + both[256:, at : at + COLS]
    real, imag = {}, {}
    for i, spec in specs.items():
        real[i] = spec[:, :width]
        imag[i] = spec[:, width:]
    power = jnp.concatenate([real[i] * real[i] + imag[i] * imag[i] for i in range(STEPS)], axis=1)
    smooth = dot(power.astype(BF), near)
    factor = lax.rsqrt(smooth * share + 1e-06)
    picked = []
    for s in range(2):
        rows = slice(s * 128, s * 128 + 128)
        scaled = [x[i][rows] * factor[rows, i * width : (i + 1) * width] for x in (real, imag) for i in range(STEPS)]
        picked.append(dot(pick, jnp.concatenate(scaled, axis=1).astype(BF)).astype(BF))
    for b in range(4):
        stacked = jnp.concatenate(
            [picked[s][b * 32 : b * 32 + 32, c * COLS : (c + 1) * COLS] for c in range(4) for s in range(2)], axis=0
        )
        out_ref[b * 16 : b * 16 + 16] = dot(mix, stacked).astype(BF).reshape(16, 16, COLS)


def in_hbm(x):
    return pltpu.with_memory_space_constraint(jnp.asarray(x), pltpu.HBM)


def whitened(raw, send_order):
    hbm = pl.BlockSpec(memory_space=pltpu.HBM)
    return pl.pallas_call(
        whiten_kernel,
        in_specs=[hbm] * 3,
        out_specs=pl.BlockSpec(memory_space=pltpu.VMEM),
        out_shape=jax.ShapeDtypeStruct((64, 16, COLS), BF),
        scratch_shapes=[
            pltpu.VMEM((2, 128, L), BF),
            pltpu.VMEM((1, 128), jnp.int32),
            pltpu.VMEM((L // 2, 2 * F), BF),
            pltpu.VMEM((2, 256, L // 2), BF),
            pltpu.VMEM((512, L // 2), BF),
            pltpu.SemaphoreType.DMA((4,)),
        ],
        compiler_params=pltpu.CompilerParams(vmem_limit_bytes=32 * 1024 * 1024),
        name="whiten",
    )(*(in_hbm(x) for x in (raw, send_order.reshape(1, 128), forward_table())))


def gather_kernel(
    own_ref, count_ref, first_hbm, offset_hbm, high_hbm, low_hbm,
    left_ref, right_ref, pick_ref, high_ref, low_ref,
    rows_ref, first_ref, offset_ref, sems,
):
    moves = ((first_hbm, first_ref), (offset_hbm, offset_ref), (high_hbm, high_ref), (low_hbm, low_ref))
    copies = [pltpu.make_async_copy(src, dst, sems.at[i]) for i, (src, dst) in enumerate(moves)]
    for copy in copies:
        copy.start()
    apart = spread_matrix(16, True)
    for b in range(4):
        block = dot(apart, own_ref[b * 16 : b * 16 + 16].reshape(256, COLS)).astype(BF)
        for c in range(4):
            for s in range(2):
                at = (c * 2 + s) * 32
                rows_ref[s, c, b * 32 : b * 32 + 32] = block[at : at + 32]
    for copy in copies[:2]:
        copy.wait()
    first = first_ref[...]
    second = first + offset_ref[...]
    slot = lax.broadcasted_iota(jnp.int32, (1, 256), 1)
    live_first = jnp.where(slot < count_ref[0], first, -1)
    at = lax.broadcasted_iota(jnp.int32, (128, 256), 0)
    left_pick = (at == live_first).astype(F32).T.astype(BF)
    right_pick = (at == second).astype(F32).T.astype(BF)
    pick_ref[...] = (at + 128 == second).astype(F32).T.astype(BF)
    for s in range(2):
        for c in range(4):
            rows = rows_ref[s, c]
            left_ref[s, c] = dot(left_pick, rows).astype(BF)
            right_ref[s, c] = dot(right_pick, rows).astype(BF)
    for copy in copies[2:]:
        copy.wait()


def gathered(own, pair_first, pair_offset, pair_count, factor):
    high, low = inverse_tables(factor)
    vmem = pl.BlockSpec(memory_space=pltpu.VMEM)
    hbm = pl.BlockSpec(memory_space=pltpu.HBM)
    rows = jax.ShapeDtypeStruct((2, 4, 256, COLS), BF)
    table = jax.ShapeDtypeStruct((2 * F, LAGS), BF)
    return pl.pallas_call(
        gather_kernel,
        in_specs=[vmem, pl.BlockSpec(memory_space=pltpu.SMEM)] + [hbm] * 4,
        out_specs=[vmem] * 5,
        out_shape=[rows, rows, jax.ShapeDtypeStruct((256, 128), BF), table, table],
        scratch_shapes=[
            pltpu.VMEM((2, 4, 128, COLS), BF),
            pltpu.VMEM((1, 256), jnp.int32),
            pltpu.VMEM((1, 256), jnp.int32),
            pltpu.SemaphoreType.DMA((4,)),
        ],
        compiler_params=pltpu.CompilerParams(vmem_limit_bytes=32 * 1024 * 1024),
        name="gather",
    )(own, pair_count, *(in_hbm(x) for x in (pair_first.reshape(1, 256), pair_offset.reshape(1, 256), high, low)))


def pairs_kernel(rim_ref, left_ref, right_ref, pick_ref, high_ref, low_ref, out_ref, rim_rows, parts_ref):
    apart = spread_matrix(8, True)
    for b in range(3):
        block = dot(apart, rim_ref[b * 8 : b * 8 + 8].reshape(128, COLS)).astype(BF)
        for c in range(4):
            for s in range(2):
                at = (c * 2 + s) * 16
                rim_rows[s, c, b * 16 : b * 16 + 16] = block[at : at + 16]
    pick = pick_ref[:, :REACH]

    def right(s, c):
        return right_ref[s, c].astype(F32) + dot(pick, rim_rows[s, c])

    for c in range(2):
        re = im = None
        for s in range(2):
            a_re, a_im = left_ref[s, c].astype(F32), left_ref[s, c + 2].astype(F32)
            c_re, c_im = right(s, c), right(s, c + 2)
            one, two = a_re * c_re + a_im * c_im, a_im * c_re - a_re * c_im
            re = one if re is None else re + one
            im = two if im is None else im + two
        for part, at in ((re, c * COLS), (im, (c + 2) * COLS)):
            parts_ref[:256, at : at + COLS], parts_ref[256:, at : at + COLS] = split(part)
    both = dot(parts_ref[...], high_ref[...])
    total = both[:256] + both[256:] + dot(parts_ref[:256], low_ref[...])
    out_ref[...] = total.astype(BF)


def pair_lags(rim, parts):
    vmem = pl.BlockSpec(memory_space=pltpu.VMEM)
    return pl.pallas_call(
        pairs_kernel,
        in_specs=[vmem] * 6,
        out_specs=vmem,
        out_shape=jax.ShapeDtypeStruct((256, LAGS), BF),
        scratch_shapes=[pltpu.VMEM((2, 4, REACH, COLS), BF), pltpu.VMEM((512, 2 * F), BF)],
        compiler_params=pltpu.CompilerParams(vmem_limit_bytes=32 * 1024 * 1024),
        name="pairs",
    )(rim, *parts)


def on_device(raw, send_order, pair_first, pair_offset, pair_count):
    seg_count = raw.shape[0]
    groups = lax.axis_size("seg")
    blocks = lax.axis_size("chan")
    sent = whitened(raw, send_order)
    own = lax.all_to_all(sent, "chan", split_axis=0, concat_axis=0, tiled=True)
    rim = lax.ppermute(own[: REACH // 2], "chan", [(i + 1, i) for i in range(blocks - 1)])
    parts = gathered(own, pair_first, pair_offset, pair_count, 1.0 / math.sqrt(seg_count * groups * F))
    lags = pair_lags(rim, parts)
    shares = lax.all_to_all(lags.reshape(groups, 256 // groups, LAGS), "seg", 0, 0, tiled=True)
    return jnp.sum(shares.astype(F32), axis=0)


def solution(mesh):
    return jax.shard_map(
        on_device,
        mesh=mesh,
        in_specs=(P("seg", "chan", None), P("chan"), P("chan"), P("chan"), P("chan")),
        out_specs=P(("chan", "seg"), None),
        check_vma=False,
    )
```

```python
import math

import jax
import jax.numpy as jnp
import numpy as np
from jax import lax
from jax.experimental import pallas as pl
from jax.experimental.pallas import tpu as pltpu
from jax.sharding import PartitionSpec as P

L = 1536
F = 512
BAND = 32
LAGS = 256
REACH = 48
COLS = 256
STEPS = 4
BF = jnp.bfloat16
F32 = jnp.float32


BINS = (1 + np.arange(STEPS)[:, None] + STEPS * np.arange(F // STEPS)[None, :]).reshape(F)


def forward_table():
    quarter = L // 4
    phase = (np.arange(quarter)[:, None] * BINS[None, :] % L).astype(np.float32) * np.float32(2.0 * math.pi / L)
    cosines = np.cos(phase).astype(BF).reshape(quarter, STEPS, F // STEPS)
    sines = (-np.sin(phase)).astype(BF).reshape(quarter, STEPS, F // STEPS)
    return np.concatenate([cosines, sines], axis=-1)[:, (0, 2, 1, 3)].reshape(quarter, 2 * F)


def inverse_tables(factor):
    bins = BINS
    lag_shift = np.arange(LAGS) - LAGS // 2
    phase = (bins[:, None] * lag_shift[None, :] % L).astype(np.float64) * (2.0 * math.pi / L)
    table = (np.concatenate([np.cos(phase), -np.sin(phase)], axis=0) * factor).astype(np.float32)
    high = table.astype(BF)
    return high, (table - high.astype(np.float32)).astype(BF)


def dot(a, b):
    return jnp.dot(a, b, preferred_element_type=F32)


def spread_matrix(blocks, back):
    rows = blocks * 16
    shape = (1, rows) if back else (rows, 1)
    mixed = lax.broadcasted_iota(jnp.int32, shape, 1 if back else 0)
    target = (mixed % 16) // 2 * (2 * blocks) + mixed // 16 * 2 + mixed % 2
    apart = lax.broadcasted_iota(jnp.int32, (rows, rows), 0 if back else 1)
    return (apart == target).astype(F32).astype(BF)


def split(x):
    high = x.astype(BF)
    return high, (x - high.astype(F32)).astype(BF)


def fold(normed, even, odd, first_row):
    quarter = L // 4
    x0, x1, x2, x3 = (normed[:, i * quarter : (i + 1) * quarter] for i in range(4))
    even0, even1 = x0 + x2, x1 + x3
    count = normed.shape[0]
    upper, lower = slice(first_row, first_row + count), slice(first_row + 256, first_row + 256 + count)
    for at, value in enumerate((even0 - even1, even0 + even1)):
        even[at, upper, :quarter], even[at, upper, quarter:] = split(value)
    for side, value in enumerate((x0 - x2, x1 - x3)):
        columns = slice(side * quarter, (side + 1) * quarter)
        odd[upper, columns], odd[lower, columns] = split(value)


def whiten_kernel(raw_hbm, order_hbm, table_hbm, out_ref, raw_ref, order_ref, table_ref, even, odd, sems):
    width = F // STEPS
    quarter = L // 4
    raw_copies = [pltpu.make_async_copy(raw_hbm.at[s], raw_ref.at[s], sems.at[3 * s]) for s in range(2)]
    table_copy = pltpu.make_async_copy(table_hbm, table_ref.at[:quarter], sems.at[1])
    order_copy = pltpu.make_async_copy(order_hbm, order_ref, sems.at[2])
    for copy in (order_copy, raw_copies[0], table_copy, raw_copies[1]):
        copy.start()
    mix = spread_matrix(16, False)

    def bin_at(position):
        return (position % width) * STEPS + position // width + 1

    bin_row = bin_at(lax.broadcasted_iota(jnp.int32, (F, 1), 0))
    bin_line = bin_at(lax.broadcasted_iota(jnp.int32, (1, F), 1))
    near = (jnp.abs(bin_row - bin_line) <= BAND).astype(F32).astype(BF)
    count = jnp.minimum(bin_line + BAND, F) - jnp.maximum(bin_line - BAND, 1) + 1
    share = 1.0 / count.astype(F32)

    order_copy.wait()
    channels = lax.broadcasted_iota(jnp.int32, (128, 128), 0)
    pick = (channels == order_ref[...]).astype(F32).T.astype(BF)
    for s in range(2):
        raw_copies[s].wait()
        for r in range(0, 128, 16):
            wave = raw_ref[s, r : r + 16].astype(F32)
            mean = jnp.sum(wave * wave, axis=-1, keepdims=True) * (1.0 / L)
            normed = (wave * lax.rsqrt(mean + 1e-05)).astype(BF).astype(F32)
            fold(normed, even, odd, s * 128 + r)
        if s == 0:
            table_copy.wait()
            for at in (2 * COLS, 3 * COLS):
                table_ref[quarter:, at : at + COLS] = table_ref[:quarter, at : at + COLS]
            for at in (0, COLS):
                cosines = table_ref[:quarter, at : at + width]
                sines = table_ref[:quarter, at + width : at + COLS]
                table_ref[quarter:, at : at + width] = sines if at == 0 else -sines
                table_ref[quarter:, at + width : at + COLS] = -cosines if at == 0 else cosines
    specs = {}
    for i in (1, 3):
        at = 2 * COLS + (i // 2) * COLS
        specs[i] = dot(even[i // 2], table_ref[:, at : at + COLS])
    both = dot(odd[...], table_ref[:, : 2 * COLS])
    for i in (0, 2):
        at = (i // 2) * COLS
        specs[i] = both[:256, at : at + COLS] + both[256:, at : at + COLS]
    real, imag = {}, {}
    for i, spec in specs.items():
        real[i] = spec[:, :width]
        imag[i] = spec[:, width:]
    power = jnp.concatenate([real[i] * real[i] + imag[i] * imag[i] for i in range(STEPS)], axis=1)
    smooth = dot(power.astype(BF), near)
    factor = lax.rsqrt(smooth * share + 1e-06)
    picked = []
    for s in range(2):
        rows = slice(s * 128, s * 128 + 128)
        scaled = [x[i][rows] * factor[rows, i * width : (i + 1) * width] for x in (real, imag) for i in range(STEPS)]
        picked.append(dot(pick, jnp.concatenate(scaled, axis=1).astype(BF)).astype(BF))
    for b in range(4):
        stacked = jnp.concatenate(
            [picked[s][b * 32 : b * 32 + 32, c * COLS : (c + 1) * COLS] for c in range(4) for s in range(2)], axis=0
        )
        out_ref[b * 16 : b * 16 + 16] = dot(mix, stacked).astype(BF).reshape(16, 16, COLS)


def in_hbm(x):
    return pltpu.with_memory_space_constraint(jnp.asarray(x), pltpu.HBM)


def whitened(raw, send_order):
    hbm = pl.BlockSpec(memory_space=pltpu.HBM)
    return pl.pallas_call(
        whiten_kernel,
        in_specs=[hbm] * 3,
        out_specs=pl.BlockSpec(memory_space=pltpu.VMEM),
        out_shape=jax.ShapeDtypeStruct((64, 16, COLS), BF),
        scratch_shapes=[
            pltpu.VMEM((2, 128, L), BF),
            pltpu.VMEM((1, 128), jnp.int32),
            pltpu.VMEM((L // 2, 2 * F), BF),
            pltpu.VMEM((2, 256, L // 2), BF),
            pltpu.VMEM((512, L // 2), BF),
            pltpu.SemaphoreType.DMA((4,)),
        ],
        compiler_params=pltpu.CompilerParams(vmem_limit_bytes=32 * 1024 * 1024),
        name="whiten",
    )(*(in_hbm(x) for x in (raw, send_order.reshape(1, 128), forward_table())))


def gather_kernel(
    own_ref, count_ref, first_hbm, offset_hbm, high_hbm, low_hbm,
    left_ref, right_ref, pick_ref, high_ref, low_ref,
    rows_ref, first_ref, offset_ref, sems,
):
    moves = ((first_hbm, first_ref), (offset_hbm, offset_ref), (high_hbm, high_ref), (low_hbm, low_ref))
    copies = [pltpu.make_async_copy(src, dst, sems.at[i]) for i, (src, dst) in enumerate(moves)]
    for copy in copies:
        copy.start()
    apart = spread_matrix(16, True)
    for b in range(4):
        block = dot(apart, own_ref[b * 16 : b * 16 + 16].reshape(256, COLS)).astype(BF)
        for c in range(4):
            for s in range(2):
                at = (c * 2 + s) * 32
                rows_ref[s, c, b * 32 : b * 32 + 32] = block[at : at + 32]
    for copy in copies[:2]:
        copy.wait()
    first = first_ref[...]
    second = first + offset_ref[...]
    slot = lax.broadcasted_iota(jnp.int32, (1, 256), 1)
    live_first = jnp.where(slot < count_ref[0], first, -1)
    at = lax.broadcasted_iota(jnp.int32, (128, 256), 0)
    left_pick = (at == live_first).astype(F32).T.astype(BF)
    right_pick = (at == second).astype(F32).T.astype(BF)
    pick_ref[...] = (at + 128 == second).astype(F32).T.astype(BF)
    for s in range(2):
        for c in range(4):
            rows = rows_ref[s, c]
            left_ref[s, c] = dot(left_pick, rows).astype(BF)
            right_ref[s, c] = dot(right_pick, rows).astype(BF)
    for copy in copies[2:]:
        copy.wait()


def gathered(own, pair_first, pair_offset, pair_count, factor):
    high, low = inverse_tables(factor)
    vmem = pl.BlockSpec(memory_space=pltpu.VMEM)
    hbm = pl.BlockSpec(memory_space=pltpu.HBM)
    rows = jax.ShapeDtypeStruct((2, 4, 256, COLS), BF)
    table = jax.ShapeDtypeStruct((2 * F, LAGS), BF)
    return pl.pallas_call(
        gather_kernel,
        in_specs=[vmem, pl.BlockSpec(memory_space=pltpu.SMEM)] + [hbm] * 4,
        out_specs=[vmem] * 5,
        out_shape=[rows, rows, jax.ShapeDtypeStruct((256, 128), BF), table, table],
        scratch_shapes=[
            pltpu.VMEM((2, 4, 128, COLS), BF),
            pltpu.VMEM((1, 256), jnp.int32),
            pltpu.VMEM((1, 256), jnp.int32),
            pltpu.SemaphoreType.DMA((4,)),
        ],
        compiler_params=pltpu.CompilerParams(vmem_limit_bytes=32 * 1024 * 1024),
        name="gather",
    )(own, pair_count, *(in_hbm(x) for x in (pair_first.reshape(1, 256), pair_offset.reshape(1, 256), high, low)))


def pairs_kernel(rim_ref, left_ref, right_ref, pick_ref, high_ref, low_ref, out_ref, rim_rows, parts_ref):
    apart = spread_matrix(8, True)
    for b in range(3):
        block = dot(apart, rim_ref[b * 8 : b * 8 + 8].reshape(128, COLS)).astype(BF)
        for c in range(4):
            for s in range(2):
                at = (c * 2 + s) * 16
                rim_rows[s, c, b * 16 : b * 16 + 16] = block[at : at + 16]
    pick = pick_ref[:, :REACH]

    def right(s, c):
        return right_ref[s, c].astype(F32) + dot(pick, rim_rows[s, c])

    for c in range(2):
        re = im = None
        for s in range(2):
            a_re, a_im = left_ref[s, c].astype(F32), left_ref[s, c + 2].astype(F32)
            c_re, c_im = right(s, c), right(s, c + 2)
            one, two = a_re * c_re + a_im * c_im, a_im * c_re - a_re * c_im
            re = one if re is None else re + one
            im = two if im is None else im + two
        for part, at in ((re, c * COLS), (im, (c + 2) * COLS)):
            parts_ref[:256, at : at + COLS], parts_ref[256:, at : at + COLS] = split(part)
    both = dot(parts_ref[...], high_ref[...])
    total = both[:256] + both[256:] + dot(parts_ref[:256], low_ref[...])
    out_ref[...] = total.astype(BF)


def pair_lags(rim, parts):
    vmem = pl.BlockSpec(memory_space=pltpu.VMEM)
    return pl.pallas_call(
        pairs_kernel,
        in_specs=[vmem] * 6,
        out_specs=vmem,
        out_shape=jax.ShapeDtypeStruct((256, LAGS), BF),
        scratch_shapes=[pltpu.VMEM((2, 4, REACH, COLS), BF), pltpu.VMEM((512, 2 * F), BF)],
        compiler_params=pltpu.CompilerParams(vmem_limit_bytes=32 * 1024 * 1024),
        name="pairs",
    )(rim, *parts)


def on_device(raw, send_order, pair_first, pair_offset, pair_count):
    seg_count = raw.shape[0]
    groups = lax.axis_size("seg")
    blocks = lax.axis_size("chan")
    sent = whitened(raw, send_order)
    own = lax.all_to_all(sent, "chan", split_axis=0, concat_axis=0, tiled=True)
    rim = lax.ppermute(own[: REACH // 2], "chan", [(i + 1, i) for i in range(blocks - 1)])
    parts = gathered(own, pair_first, pair_offset, pair_count, 1.0 / math.sqrt(seg_count * groups * F))
    lags = pair_lags(rim, parts)
    shares = lax.all_to_all(lags.reshape(groups, 256 // groups, LAGS), "seg", 0, 0, tiled=True)
    return jnp.sum(shares.astype(F32), axis=0)


def solution(mesh):
    return jax.shard_map(
        on_device,
        mesh=mesh,
        in_specs=(P("seg", "chan", None), P("chan"), P("chan"), P("chan"), P("chan")),
        out_specs=P(("chan", "seg"), None),
        check_vma=False,
    )
```

```python
import math

import jax
import jax.numpy as jnp
import numpy as np
from jax import lax
from jax.experimental import pallas as pl
from jax.experimental.pallas import tpu as pltpu
from jax.sharding import PartitionSpec as P

L = 1536
F = 512
BAND = 32
LAGS = 256
REACH = 48
COLS = 256
STEPS = 4
BF = jnp.bfloat16
F32 = jnp.float32


BINS = (1 + np.arange(STEPS)[:, None] + STEPS * np.arange(F // STEPS)[None, :]).reshape(F)


def forward_table():
    quarter = L // 4
    phase = (np.arange(quarter)[:, None] * BINS[None, :] % L).astype(np.float32) * np.float32(2.0 * math.pi / L)
    cosines = np.cos(phase).astype(BF).reshape(quarter, STEPS, F // STEPS)
    sines = (-np.sin(phase)).astype(BF).reshape(quarter, STEPS, F // STEPS)
    return np.concatenate([cosines, sines], axis=-1)[:, (0, 2, 1, 3)].reshape(quarter, 2 * F)


def inverse_tables(factor):
    bins = BINS
    lag_shift = np.arange(LAGS) - LAGS // 2
    phase = (bins[:, None] * lag_shift[None, :] % L).astype(np.float64) * (2.0 * math.pi / L)
    table = (np.concatenate([np.cos(phase), -np.sin(phase)], axis=0) * factor).astype(np.float32)
    high = table.astype(BF)
    return high, (table - high.astype(np.float32)).astype(BF)


def dot(a, b):
    return jnp.dot(a, b, preferred_element_type=F32)


def spread_matrix(blocks, back):
    rows = blocks * 16
    shape = (1, rows) if back else (rows, 1)
    mixed = lax.broadcasted_iota(jnp.int32, shape, 1 if back else 0)
    target = (mixed % 16) // 2 * (2 * blocks) + mixed // 16 * 2 + mixed % 2
    apart = lax.broadcasted_iota(jnp.int32, (rows, rows), 0 if back else 1)
    return (apart == target).astype(F32).astype(BF)


def split(x):
    high = x.astype(BF)
    return high, (x - high.astype(F32)).astype(BF)


def fold(normed, even, odd, first_row):
    quarter = L // 4
    x0, x1, x2, x3 = (normed[:, i * quarter : (i + 1) * quarter] for i in range(4))
    even0, even1 = x0 + x2, x1 + x3
    count = normed.shape[0]
    upper, lower = slice(first_row, first_row + count), slice(first_row + 256, first_row + 256 + count)
    for at, value in enumerate((even0 - even1, even0 + even1)):
        even[at, upper, :quarter], even[at, upper, quarter:] = split(value)
    for side, value in enumerate((x0 - x2, x1 - x3)):
        columns = slice(side * quarter, (side + 1) * quarter)
        odd[upper, columns], odd[lower, columns] = split(value)


def whiten_kernel(raw_hbm, order_hbm, table_hbm, out_ref, raw_ref, order_ref, table_ref, even, odd, sems):
    width = F // STEPS
    quarter = L // 4
    raw_copies = [pltpu.make_async_copy(raw_hbm.at[s], raw_ref.at[s], sems.at[3 * s]) for s in range(2)]
    table_copy = pltpu.make_async_copy(table_hbm, table_ref.at[:quarter], sems.at[1])
    order_copy = pltpu.make_async_copy(order_hbm, order_ref, sems.at[2])
    for copy in (order_copy, raw_copies[0], table_copy, raw_copies[1]):
        copy.start()
    mix = spread_matrix(16, False)

    def bin_at(position):
        return (position % width) * STEPS + position // width + 1

    bin_row = bin_at(lax.broadcasted_iota(jnp.int32, (F, 1), 0))
    bin_line = bin_at(lax.broadcasted_iota(jnp.int32, (1, F), 1))
    near = (jnp.abs(bin_row - bin_line) <= BAND).astype(F32).astype(BF)
    count = jnp.minimum(bin_line + BAND, F) - jnp.maximum(bin_line - BAND, 1) + 1
    share = 1.0 / count.astype(F32)

    order_copy.wait()
    channels = lax.broadcasted_iota(jnp.int32, (128, 128), 0)
    pick = (channels == order_ref[...]).astype(F32).T.astype(BF)
    for s in range(2):
        raw_copies[s].wait()
        for r in range(0, 128, 16):
            wave = raw_ref[s, r : r + 16].astype(F32)
            mean = jnp.sum(wave * wave, axis=-1, keepdims=True) * (1.0 / L)
            normed = (wave * lax.rsqrt(mean + 1e-05)).astype(BF).astype(F32)
            fold(normed, even, odd, s * 128 + r)
        if s == 0:
            table_copy.wait()
            for at in (2 * COLS, 3 * COLS):
                table_ref[quarter:, at : at + COLS] = table_ref[:quarter, at : at + COLS]
            for at in (0, COLS):
                cosines = table_ref[:quarter, at : at + width]
                sines = table_ref[:quarter, at + width : at + COLS]
                table_ref[quarter:, at : at + width] = sines if at == 0 else -sines
                table_ref[quarter:, at + width : at + COLS] = -cosines if at == 0 else cosines
    specs = {}
    for i in (1, 3):
        at = 2 * COLS + (i // 2) * COLS
        specs[i] = dot(even[i // 2], table_ref[:, at : at + COLS])
    both = dot(odd[...], table_ref[:, : 2 * COLS])
    for i in (0, 2):
        at = (i // 2) * COLS
        specs[i] = both[:256, at : at + COLS] + both[256:, at : at + COLS]
    real, imag = {}, {}
    for i, spec in specs.items():
        real[i] = spec[:, :width]
        imag[i] = spec[:, width:]
    power = jnp.concatenate([real[i] * real[i] + imag[i] * imag[i] for i in range(STEPS)], axis=1)
    smooth = dot(power.astype(BF), near)
    factor = lax.rsqrt(smooth * share + 1e-06)
    picked = []
    for s in range(2):
        rows = slice(s * 128, s * 128 + 128)
        scaled = [x[i][rows] * factor[rows, i * width : (i + 1) * width] for x in (real, imag) for i in range(STEPS)]
        picked.append(dot(pick, jnp.concatenate(scaled, axis=1).astype(BF)).astype(BF))
    for b in range(4):
        stacked = jnp.concatenate(
            [picked[s][b * 32 : b * 32 + 32, c * COLS : (c + 1) * COLS] for c in range(4) for s in range(2)], axis=0
        )
        out_ref[b * 16 : b * 16 + 16] = dot(mix, stacked).astype(BF).reshape(16, 16, COLS)


def in_hbm(x):
    return pltpu.with_memory_space_constraint(jnp.asarray(x), pltpu.HBM)


def whitened(raw, send_order):
    hbm = pl.BlockSpec(memory_space=pltpu.HBM)
    return pl.pallas_call(
        whiten_kernel,
        in_specs=[hbm] * 3,
        out_specs=pl.BlockSpec(memory_space=pltpu.VMEM),
        out_shape=jax.ShapeDtypeStruct((64, 16, COLS), BF),
        scratch_shapes=[
            pltpu.VMEM((2, 128, L), BF),
            pltpu.VMEM((1, 128), jnp.int32),
            pltpu.VMEM((L // 2, 2 * F), BF),
            pltpu.VMEM((2, 256, L // 2), BF),
            pltpu.VMEM((512, L // 2), BF),
            pltpu.SemaphoreType.DMA((4,)),
        ],
        compiler_params=pltpu.CompilerParams(vmem_limit_bytes=32 * 1024 * 1024),
        name="whiten",
    )(*(in_hbm(x) for x in (raw, send_order.reshape(1, 128), forward_table())))


def gather_kernel(
    own_ref, count_ref, first_hbm, offset_hbm, high_hbm, low_hbm,
    left_ref, rows_ref, pick_ref, high_ref, low_ref,
    first_ref, offset_ref, sems,
):
    moves = ((first_hbm, first_ref), (offset_hbm, offset_ref), (high_hbm, high_ref), (low_hbm, low_ref))
    copies = [pltpu.make_async_copy(src, dst, sems.at[i]) for i, (src, dst) in enumerate(moves)]
    for copy in copies:
        copy.start()
    apart = spread_matrix(16, True)
    for b in range(4):
        block = dot(apart, own_ref[b * 16 : b * 16 + 16].reshape(256, COLS)).astype(BF)
        for c in range(4):
            for s in range(2):
                at = (c * 2 + s) * 32
                rows_ref[s, c, b * 32 : b * 32 + 32] = block[at : at + 32]
    for copy in copies[:2]:
        copy.wait()
    first = first_ref[...]
    second = first + offset_ref[...]
    slot = lax.broadcasted_iota(jnp.int32, (1, 256), 1)
    live_first = jnp.where(slot < count_ref[0], first, -1)
    at = lax.broadcasted_iota(jnp.int32, (128, 256), 0)
    left_pick = (at == live_first).astype(F32).T.astype(BF)
    any_at = lax.broadcasted_iota(jnp.int32, (128 + REACH, 256), 0)
    pick_ref[...] = (any_at == second).astype(F32).T.astype(BF)
    for s in range(2):
        for c in range(4):
            left_ref[s, c] = dot(left_pick, rows_ref[s, c]).astype(BF)
    for copy in copies[2:]:
        copy.wait()


def gathered(own, pair_first, pair_offset, pair_count, factor):
    high, low = inverse_tables(factor)
    vmem = pl.BlockSpec(memory_space=pltpu.VMEM)
    hbm = pl.BlockSpec(memory_space=pltpu.HBM)
    left = jax.ShapeDtypeStruct((2, 4, 256, COLS), BF)
    rows = jax.ShapeDtypeStruct((2, 4, 128, COLS), BF)
    table = jax.ShapeDtypeStruct((2 * F, LAGS), BF)
    return pl.pallas_call(
        gather_kernel,
        in_specs=[vmem, pl.BlockSpec(memory_space=pltpu.SMEM)] + [hbm] * 4,
        out_specs=[vmem] * 5,
        out_shape=[left, rows, jax.ShapeDtypeStruct((256, 128 + REACH), BF), table, table],
        scratch_shapes=[
            pltpu.VMEM((1, 256), jnp.int32),
            pltpu.VMEM((1, 256), jnp.int32),
            pltpu.SemaphoreType.DMA((4,)),
        ],
        compiler_params=pltpu.CompilerParams(vmem_limit_bytes=32 * 1024 * 1024),
        name="gather",
    )(own, pair_count, *(in_hbm(x) for x in (pair_first.reshape(1, 256), pair_offset.reshape(1, 256), high, low)))


def pairs_kernel(rim_ref, left_ref, own_ref, pick_ref, high_ref, low_ref, out_ref, rows_ref, parts_ref):
    apart = spread_matrix(8, True)
    for b in range(3):
        block = dot(apart, rim_ref[b * 8 : b * 8 + 8].reshape(128, COLS)).astype(BF)
        for c in range(4):
            for s in range(2):
                at = (c * 2 + s) * 16
                rows_ref[s, c, 128 + b * 16 : 144 + b * 16] = block[at : at + 16]
    rows_ref[:, :, :128] = own_ref[...]
    pick = pick_ref[...]

    def right(s, c):
        return dot(pick, rows_ref[s, c])

    for c in range(2):
        re = im = None
        for s in range(2):
            a_re, a_im = left_ref[s, c].astype(F32), left_ref[s, c + 2].astype(F32)
            c_re, c_im = right(s, c), right(s, c + 2)
            one, two = a_re * c_re + a_im * c_im, a_im * c_re - a_re * c_im
            re = one if re is None else re + one
            im = two if im is None else im + two
        for part, at in ((re, c * COLS), (im, (c + 2) * COLS)):
            parts_ref[:256, at : at + COLS], parts_ref[256:, at : at + COLS] = split(part)
    both = dot(parts_ref[...], high_ref[...])
    total = both[:256] + both[256:] + dot(parts_ref[:256], low_ref[...])
    out_ref[...] = total.astype(BF)


def pair_lags(rim, parts):
    vmem = pl.BlockSpec(memory_space=pltpu.VMEM)
    return pl.pallas_call(
        pairs_kernel,
        in_specs=[vmem] * 6,
        out_specs=vmem,
        out_shape=jax.ShapeDtypeStruct((256, LAGS), BF),
        scratch_shapes=[pltpu.VMEM((2, 4, 128 + REACH, COLS), BF), pltpu.VMEM((512, 2 * F), BF)],
        compiler_params=pltpu.CompilerParams(vmem_limit_bytes=32 * 1024 * 1024),
        name="pairs",
    )(rim, *parts)


def on_device(raw, send_order, pair_first, pair_offset, pair_count):
    seg_count = raw.shape[0]
    groups = lax.axis_size("seg")
    blocks = lax.axis_size("chan")
    sent = whitened(raw, send_order)
    own = lax.all_to_all(sent, "chan", split_axis=0, concat_axis=0, tiled=True)
    rim = lax.ppermute(own[: REACH // 2], "chan", [(i + 1, i) for i in range(blocks - 1)])
    parts = gathered(own, pair_first, pair_offset, pair_count, 1.0 / math.sqrt(seg_count * groups * F))
    lags = pair_lags(rim, parts)
    shares = lax.all_to_all(lags.reshape(groups, 256 // groups, LAGS), "seg", 0, 0, tiled=True)
    return jnp.sum(shares.astype(F32), axis=0)


def solution(mesh):
    return jax.shard_map(
        on_device,
        mesh=mesh,
        in_specs=(P("seg", "chan", None), P("chan"), P("chan"), P("chan"), P("chan")),
        out_specs=P(("chan", "seg"), None),
        check_vma=False,
    )
```

```python
import math

import jax
import jax.numpy as jnp
import numpy as np
from jax import lax
from jax.experimental import pallas as pl
from jax.experimental.pallas import tpu as pltpu
from jax.sharding import PartitionSpec as P

L = 1536
F = 512
BAND = 32
LAGS = 256
REACH = 48
COLS = 256
STEPS = 4
BF = jnp.bfloat16
F32 = jnp.float32


BINS = (1 + np.arange(STEPS)[:, None] + STEPS * np.arange(F // STEPS)[None, :]).reshape(F)


def forward_table():
    quarter = L // 4
    phase = (np.arange(quarter)[:, None] * BINS[None, :] % L).astype(np.float32) * np.float32(2.0 * math.pi / L)
    cosines = np.cos(phase).astype(BF).reshape(quarter, STEPS, F // STEPS)
    sines = (-np.sin(phase)).astype(BF).reshape(quarter, STEPS, F // STEPS)
    return np.concatenate([cosines, sines], axis=-1)[:, (0, 2, 1, 3)].reshape(quarter, 2 * F)


def inverse_tables(factor):
    bins = BINS
    lag_shift = np.arange(LAGS) - LAGS // 2
    phase = (bins[:, None] * lag_shift[None, :] % L).astype(np.float64) * (2.0 * math.pi / L)
    table = (np.concatenate([np.cos(phase), -np.sin(phase)], axis=0) * factor).astype(np.float32)
    high = table.astype(BF)
    return high, (table - high.astype(np.float32)).astype(BF)


def dot(a, b):
    return jnp.dot(a, b, preferred_element_type=F32)


def spread_matrix(blocks, back):
    rows = blocks * 16
    shape = (1, rows) if back else (rows, 1)
    mixed = lax.broadcasted_iota(jnp.int32, shape, 1 if back else 0)
    target = (mixed % 16) // 2 * (2 * blocks) + mixed // 16 * 2 + mixed % 2
    apart = lax.broadcasted_iota(jnp.int32, (rows, rows), 0 if back else 1)
    return (apart == target).astype(F32).astype(BF)


def split(x):
    high = x.astype(BF)
    return high, (x - high.astype(F32)).astype(BF)


def fold(normed, even, odd, first_row):
    quarter = L // 4
    x0, x1, x2, x3 = (normed[:, i * quarter : (i + 1) * quarter] for i in range(4))
    even0, even1 = x0 + x2, x1 + x3
    count = normed.shape[0]
    upper, lower = slice(first_row, first_row + count), slice(first_row + 256, first_row + 256 + count)
    for at, value in enumerate((even0 - even1, even0 + even1)):
        even[at, upper, :quarter], even[at, upper, quarter:] = split(value)
    for side, value in enumerate((x0 - x2, x1 - x3)):
        columns = slice(side * quarter, (side + 1) * quarter)
        odd[upper, columns], odd[lower, columns] = split(value)


def whiten_kernel(raw_hbm, order_hbm, table_hbm, out_ref, raw_ref, order_ref, table_ref, even, odd, sems):
    width = F // STEPS
    quarter = L // 4
    raw_copies = [pltpu.make_async_copy(raw_hbm.at[s], raw_ref.at[s], sems.at[3 * s]) for s in range(2)]
    table_copy = pltpu.make_async_copy(table_hbm, table_ref.at[:quarter], sems.at[1])
    order_copy = pltpu.make_async_copy(order_hbm, order_ref, sems.at[2])
    for copy in (order_copy, raw_copies[0], table_copy, raw_copies[1]):
        copy.start()
    mix = spread_matrix(16, False)

    def bin_at(position):
        return (position % width) * STEPS + position // width + 1

    bin_row = bin_at(lax.broadcasted_iota(jnp.int32, (F, 1), 0))
    bin_line = bin_at(lax.broadcasted_iota(jnp.int32, (1, F), 1))
    near = (jnp.abs(bin_row - bin_line) <= BAND).astype(F32).astype(BF)
    count = jnp.minimum(bin_line + BAND, F) - jnp.maximum(bin_line - BAND, 1) + 1
    share = 1.0 / count.astype(F32)

    order_copy.wait()
    channels = lax.broadcasted_iota(jnp.int32, (128, 128), 0)
    pick = (channels == order_ref[...]).astype(F32).T.astype(BF)
    for s in range(2):
        raw_copies[s].wait()
        for r in range(0, 128, 16):
            wave = raw_ref[s, r : r + 16].astype(F32)
            mean = jnp.sum(wave * wave, axis=-1, keepdims=True) * (1.0 / L)
            normed = (wave * lax.rsqrt(mean + 1e-05)).astype(BF).astype(F32)
            fold(normed, even, odd, s * 128 + r)
        if s == 0:
            table_copy.wait()
            for at in (2 * COLS, 3 * COLS):
                table_ref[quarter:, at : at + COLS] = table_ref[:quarter, at : at + COLS]
            for at in (0, COLS):
                cosines = table_ref[:quarter, at : at + width]
                sines = table_ref[:quarter, at + width : at + COLS]
                table_ref[quarter:, at : at + width] = sines if at == 0 else -sines
                table_ref[quarter:, at + width : at + COLS] = -cosines if at == 0 else cosines
    specs = {}
    for i in (1, 3):
        at = 2 * COLS + (i // 2) * COLS
        specs[i] = dot(even[i // 2], table_ref[:, at : at + COLS])
    both = dot(odd[...], table_ref[:, : 2 * COLS])
    for i in (0, 2):
        at = (i // 2) * COLS
        specs[i] = both[:256, at : at + COLS] + both[256:, at : at + COLS]
    real, imag = {}, {}
    for i, spec in specs.items():
        real[i] = spec[:, :width]
        imag[i] = spec[:, width:]
    power = jnp.concatenate([real[i] * real[i] + imag[i] * imag[i] for i in range(STEPS)], axis=1)
    smooth = dot(power.astype(BF), near)
    factor = lax.rsqrt(smooth * share + 1e-06)
    picked = []
    for s in range(2):
        rows = slice(s * 128, s * 128 + 128)
        scaled = [x[i][rows] * factor[rows, i * width : (i + 1) * width] for x in (real, imag) for i in range(STEPS)]
        picked.append(dot(pick, jnp.concatenate(scaled, axis=1).astype(BF)).astype(BF))
    for b in range(4):
        stacked = jnp.concatenate(
            [picked[s][b * 32 : b * 32 + 32, c * COLS : (c + 1) * COLS] for c in range(4) for s in range(2)], axis=0
        )
        out_ref[b * 16 : b * 16 + 16] = dot(mix, stacked).astype(BF).reshape(16, 16, COLS)


def in_hbm(x):
    return pltpu.with_memory_space_constraint(jnp.asarray(x), pltpu.HBM)


def whitened(raw, send_order):
    hbm = pl.BlockSpec(memory_space=pltpu.HBM)
    return pl.pallas_call(
        whiten_kernel,
        in_specs=[hbm] * 3,
        out_specs=pl.BlockSpec(memory_space=pltpu.VMEM),
        out_shape=jax.ShapeDtypeStruct((64, 16, COLS), BF),
        scratch_shapes=[
            pltpu.VMEM((2, 128, L), BF),
            pltpu.VMEM((1, 128), jnp.int32),
            pltpu.VMEM((L // 2, 2 * F), BF),
            pltpu.VMEM((2, 256, L // 2), BF),
            pltpu.VMEM((512, L // 2), BF),
            pltpu.SemaphoreType.DMA((4,)),
        ],
        compiler_params=pltpu.CompilerParams(vmem_limit_bytes=32 * 1024 * 1024),
        name="whiten",
    )(*(in_hbm(x) for x in (raw, send_order.reshape(1, 128), forward_table())))


def gather_kernel(
    own_ref, count_ref, first_hbm, offset_hbm, high_hbm, low_hbm,
    left_ref, rows_ref, pick_ref, high_ref, low_ref,
    first_ref, offset_ref, sems,
):
    moves = ((first_hbm, first_ref), (offset_hbm, offset_ref), (high_hbm, high_ref), (low_hbm, low_ref))
    copies = [pltpu.make_async_copy(src, dst, sems.at[i]) for i, (src, dst) in enumerate(moves)]
    for copy in copies:
        copy.start()
    apart = spread_matrix(16, True)
    for b in range(4):
        block = dot(apart, own_ref[b * 16 : b * 16 + 16].reshape(256, COLS)).astype(BF)
        for c in range(4):
            for s in range(2):
                at = (c * 2 + s) * 32
                rows_ref[s, c, b * 32 : b * 32 + 32] = block[at : at + 32]
    for copy in copies[:2]:
        copy.wait()
    first = first_ref[...]
    second = first + offset_ref[...]
    slot = lax.broadcasted_iota(jnp.int32, (1, 256), 1)
    live_first = jnp.where(slot < count_ref[0], first, -1)
    at = lax.broadcasted_iota(jnp.int32, (128, 256), 0)
    left_pick = (at == live_first).astype(F32).T.astype(BF)
    any_at = lax.broadcasted_iota(jnp.int32, (128 + REACH, 256), 0)
    pick_ref[...] = (any_at == second).astype(F32).T.astype(BF)
    for s in range(2):
        for c in range(4):
            left_ref[s, c] = dot(left_pick, rows_ref[s, c])
    for copy in copies[2:]:
        copy.wait()


def gathered(own, pair_first, pair_offset, pair_count, factor):
    high, low = inverse_tables(factor)
    vmem = pl.BlockSpec(memory_space=pltpu.VMEM)
    hbm = pl.BlockSpec(memory_space=pltpu.HBM)
    left = jax.ShapeDtypeStruct((2, 4, 256, COLS), F32)
    rows = jax.ShapeDtypeStruct((2, 4, 128, COLS), BF)
    table = jax.ShapeDtypeStruct((2 * F, LAGS), BF)
    return pl.pallas_call(
        gather_kernel,
        in_specs=[vmem, pl.BlockSpec(memory_space=pltpu.SMEM)] + [hbm] * 4,
        out_specs=[vmem] * 5,
        out_shape=[left, rows, jax.ShapeDtypeStruct((256, 128 + REACH), BF), table, table],
        scratch_shapes=[
            pltpu.VMEM((1, 256), jnp.int32),
            pltpu.VMEM((1, 256), jnp.int32),
            pltpu.SemaphoreType.DMA((4,)),
        ],
        compiler_params=pltpu.CompilerParams(vmem_limit_bytes=32 * 1024 * 1024),
        name="gather",
    )(own, pair_count, *(in_hbm(x) for x in (pair_first.reshape(1, 256), pair_offset.reshape(1, 256), high, low)))


def pairs_kernel(rim_ref, left_ref, own_ref, pick_ref, high_ref, low_ref, out_ref, rows_ref, parts_ref):
    apart = spread_matrix(8, True)
    for b in range(3):
        block = dot(apart, rim_ref[b * 8 : b * 8 + 8].reshape(128, COLS)).astype(BF)
        for c in range(4):
            for s in range(2):
                at = (c * 2 + s) * 16
                rows_ref[s, c, 128 + b * 16 : 144 + b * 16] = block[at : at + 16]
    rows_ref[:, :, :128] = own_ref[...]
    pick = pick_ref[...]

    def right(s, c):
        return dot(pick, rows_ref[s, c])

    for c in range(2):
        re = im = None
        for s in range(2):
            a_re, a_im = left_ref[s, c], left_ref[s, c + 2]
            c_re, c_im = right(s, c), right(s, c + 2)
            one, two = a_re * c_re + a_im * c_im, a_im * c_re - a_re * c_im
            re = one if re is None else re + one
            im = two if im is None else im + two
        for part, at in ((re, c * COLS), (im, (c + 2) * COLS)):
            parts_ref[:256, at : at + COLS], parts_ref[256:, at : at + COLS] = split(part)
    both = dot(parts_ref[...], high_ref[...])
    total = both[:256] + both[256:] + dot(parts_ref[:256], low_ref[...])
    out_ref[...] = total.astype(BF)


def pair_lags(rim, parts):
    vmem = pl.BlockSpec(memory_space=pltpu.VMEM)
    return pl.pallas_call(
        pairs_kernel,
        in_specs=[vmem] * 6,
        out_specs=vmem,
        out_shape=jax.ShapeDtypeStruct((256, LAGS), BF),
        scratch_shapes=[pltpu.VMEM((2, 4, 128 + REACH, COLS), BF), pltpu.VMEM((512, 2 * F), BF)],
        compiler_params=pltpu.CompilerParams(vmem_limit_bytes=32 * 1024 * 1024),
        name="pairs",
    )(rim, *parts)


def on_device(raw, send_order, pair_first, pair_offset, pair_count):
    seg_count = raw.shape[0]
    groups = lax.axis_size("seg")
    blocks = lax.axis_size("chan")
    sent = whitened(raw, send_order)
    own = lax.all_to_all(sent, "chan", split_axis=0, concat_axis=0, tiled=True)
    rim = lax.ppermute(own[: REACH // 2], "chan", [(i + 1, i) for i in range(blocks - 1)])
    parts = gathered(own, pair_first, pair_offset, pair_count, 1.0 / math.sqrt(seg_count * groups * F))
    lags = pair_lags(rim, parts)
    shares = lax.all_to_all(lags.reshape(groups, 256 // groups, LAGS), "seg", 0, 0, tiled=True)
    return jnp.sum(shares.astype(F32), axis=0)


def solution(mesh):
    return jax.shard_map(
        on_device,
        mesh=mesh,
        in_specs=(P("seg", "chan", None), P("chan"), P("chan"), P("chan"), P("chan")),
        out_specs=P(("chan", "seg"), None),
        check_vma=False,
    )
```
